32 devices in a mesh: band: 2 (over x), row: 16 (over z, y, core).
Axes of the slice: x: 2, y: 2, z: 4, core: 2. Of those that a mesh axis runs over, the one named last changes fastest.
Arguments:
- prior_cov: float32 [16384, 8192], P(('band', 'row')), parts along dimension 0, as said below
- snapshots: bfloat16 [2, 16384, 256], P(None, ('band', 'row')), parts along dimension 1, may hold values from -6 to 6
- prior_basis: float32 [16384, 128], P(('band', 'row')), parts along dimension 0, may hold values from -0.0625 to 0.0625
Outputs:
- new_cov: float32 [16384, 8192], P(('band', 'row')), parts along dimension 0
- new_basis: float32 [16384, 128], P(('band', 'row')), parts along dimension 0
The draws below stay inside these ranges and needn't reach their ends.
There are 2 independent parts, one for each index of `band`. The reference program is written for one: setup_inputs(seed, part) draws one part's arguments, and reference() takes and returns one part's arrays. A program takes and returns all parts, laid end to end along the dimension named above; each array names one. Nothing has to cross between parts.
Inputs may be any that keep to these rules, and one draw needn't show every extreme that they name: prior_cov is symmetric and positive definite.
All inputs are finite; a program needn't handle non-finite values.
Results may differ from the reference program's by a relative error of at most 0.0003.
Values may be sent and summed in bfloat16 or wider, within the bound.
No kernel may reach another device: no remote copies, remote signals or barrier semaphores. Data moves between devices by JAX's collectives and lax.ppermute only.
A program may use at most 128 MiB of HBM per device.

```python
import math
import jax
import jax.numpy as jnp
from jax import lax

ORDER = 8192
SNAP = 256
RANK = 128
WINDOWS = 2


def draw_prior_cov(key, part):
    key = jax.random.fold_in(key, 11)
    noise_key, scale_key = jax.random.split(key)
    noise = jax.random.normal(noise_key, (ORDER, ORDER), jnp.float32)
    scales = jnp.exp(jax.random.uniform(scale_key, (ORDER,), jnp.float32, 0.0, math.log(math.sqrt(10.0))))
    symmetric = (noise + noise.T) * (0.9 / math.sqrt(2.0 * ORDER))
    inner = symmetric + 3.0 * jnp.eye(ORDER, dtype=jnp.float32)
    outer_scale = scales[:, None] * scales[None, :]
    return inner * outer_scale


def block_levels(stream_key, dims, shards, smallest, high):
    factor_of, own = 1.0, jax.random.fold_in(stream_key, 6)
    for axis_at, shards_of in shards:
        steps = jnp.exp(jax.random.uniform(jax.random.fold_in(own, axis_at), (shards_of,), jnp.float32, smallest / len(shards), high / len(shards)))
        factor_of = factor_of * jnp.repeat(steps, dims[axis_at] // shards_of).reshape([-1 if axis == axis_at else 1 for axis in range(len(dims))])
    return factor_of


def normal_values(key, dims, deviation, most, pieces=(), kind=jnp.bfloat16):
    loudness = block_levels(key, dims, pieces, -0.22, 0.18) if pieces else 1.0
    entries = jax.random.normal(key, dims, jnp.float32) * deviation * loudness
    return jnp.minimum(jnp.maximum(entries, -most), most).astype(kind)


def setup_inputs(seed: int = 0, part: int = 0) -> dict:
    arg_keys = jax.random.split(jax.random.key(seed), 4)
    part_splits = jax.random.split(jax.random.fold_in(arg_keys[3], part), 4)
    return {
        "prior_cov": draw_prior_cov(jax.random.fold_in(jax.random.fold_in(arg_keys[3], part), 71), part),
        "snapshots": normal_values(part_splits[1], (WINDOWS, ORDER, SNAP), 1.0, 6.0, ((1, 16),)),
        "prior_basis": normal_values(part_splits[2], (ORDER, RANK), ORDER ** -0.5, 0.0625, ((0, 16),), jnp.float32),
    }


forget_factor = 0.9

def reference(prior_cov, snapshots, prior_basis):
    covariance = prior_cov
    subspace = prior_basis
    for window in range(WINDOWS):
        snapshot_panel = snapshots[window]
        outer_term = jnp.dot(snapshot_panel.astype(jnp.float32), snapshot_panel.T.astype(jnp.float32), preferred_element_type=jnp.float32)
        covariance = forget_factor * covariance + outer_term * (1.0 / SNAP)
        applied = jnp.dot(covariance.astype(jnp.float32), subspace.astype(jnp.float32), precision=lax.Precision.HIGHEST, preferred_element_type=jnp.float32)
        gram_matrix = jnp.dot(applied.T.astype(jnp.float32), applied.astype(jnp.float32), precision=lax.Precision.HIGHEST, preferred_element_type=jnp.float32)
        lower_factor = jnp.linalg.cholesky(gram_matrix)
        subspace = lax.linalg.triangular_solve(lower_factor, applied, left_side=False, lower=True, transpose_a=True)
    return (covariance, subspace)
```

```python
import functools

import jax
import jax.numpy as jnp
from jax import lax
from jax.experimental import pallas as pl
from jax.experimental.pallas import tpu as pltpu
from jax.sharding import PartitionSpec as P

forget_factor = 0.9
pad_rows = 16
any_space = pl.BlockSpec(memory_space=pl.ANY)
in_vmem = pl.BlockSpec(memory_space=pltpu.VMEM)
in_smem = pl.BlockSpec(memory_space=pltpu.SMEM)
params = pltpu.CompilerParams(vmem_limit_bytes=40 * 2**20)

inner = (((1,), (0,)), ((), ()))
lead = (((0,), (0,)), ((), ()))
trail = (((1,), (1,)), ((), ()))


def dot(a, b, dims):
    return lax.dot_general(a, b, dims, preferred_element_type=jnp.float32)


def split(x):
    high = x.astype(jnp.bfloat16)
    return high, (x - high.astype(jnp.float32)).astype(jnp.bfloat16)


def dot3(a, b, dims):
    a_high, a_low = split(a)
    b_high, b_low = split(b)
    return dot(a_high, b_high, dims) + (dot(a_high, b_low, dims) + dot(a_low, b_high, dims))


def dot2(a, b, dims):
    b_high, b_low = split(b)
    return dot(a, b_high, dims) + dot(a, b_low, dims)


def chip_at(position, chips):
    position = position % chips
    return jnp.where(position < chips // 2, 2 * position, 2 * (chips - 1 - position) + 1)


def position_of(chip, chips):
    return jnp.where(chip % 2 == 0, chip // 2, chips - 1 - chip // 2)


def ring_pairs(devices, way):
    chips = devices // 2
    order = list(range(0, chips, 2)) + list(range(chips - 1, 0, -2))
    pairs = []
    for at in range(chips):
        for core in range(2):
            pairs.append((2 * order[at] + core, 2 * order[(at + way) % chips] + core))
    return pairs


def partner_pairs(devices, mask):
    return [(i, i ^ mask) for i in range(devices)]


def ring_gather(block, devices, axis):
    chips = devices // 2
    forth, back = ring_pairs(devices, 1), ring_pairs(devices, -1)
    swap = partner_pairs(devices, 1)
    groups = [[block, lax.ppermute(block, "row", swap)]]
    ahead = behind = block
    for step in range(1, chips // 2):
        ahead = lax.ppermute(ahead, "row", forth)
        behind = lax.ppermute(behind, "row", back)
        groups.append(
            [ahead, lax.ppermute(ahead, "row", swap), behind, lax.ppermute(behind, "row", swap)]
        )
    half = block.shape[axis] // 2
    ahead = lax.ppermute(lax.slice_in_dim(ahead, 0, half, axis=axis), "row", forth)
    behind = lax.ppermute(lax.slice_in_dim(behind, half, 2 * half, axis=axis), "row", back)
    groups.append(
        [ahead, lax.ppermute(ahead, "row", swap), behind, lax.ppermute(behind, "row", swap)]
    )
    return groups


def ring_offsets(devices, rows):
    me = lax.axis_index("row")
    chips, core = devices // 2, me % 2
    at = position_of(me // 2, chips)
    groups = [[me * rows, (me ^ 1) * rows]]
    for step in range(1, chips // 2):
        group = []
        for there in (at - step, at + step):
            chip = chip_at(there + chips, chips)
            group += [(2 * chip + core) * rows, (2 * chip + 1 - core) * rows]
        groups.append(group)
    chip = chip_at(at + chips // 2, chips)
    own, other = (2 * chip + core) * rows, (2 * chip + 1 - core) * rows
    groups.append([own, other, own + rows // 2, other + rows // 2])
    return groups


def total_over_row(part, devices):
    half = part.shape[0] // 2
    core = lax.axis_index("row") % 2
    swap = partner_pairs(devices, 1)
    mine = lax.dynamic_slice_in_dim(part, core * half, half, axis=0)
    theirs = lax.dynamic_slice_in_dim(part, (1 - core) * half, half, axis=0)
    mine = mine + lax.ppermute(theirs, "row", swap)
    mask = 2
    while mask < devices:
        mine = mine + lax.ppermute(mine, "row", partner_pairs(devices, mask))
        mask *= 2
    theirs = lax.ppermute(mine, "row", swap)
    first = jnp.where(core == 0, mine, theirs)
    second = jnp.where(core == 0, theirs, mine)
    return jnp.concatenate([first, second], axis=0)


def prepare(offset, prior_cov, snapshot_panel, basis):
    rows, count = snapshot_panel.shape
    rank = basis.shape[1]

    def kernel(offset_ref, cov_ref, snap_ref, basis_ref, out_ref, corner, sem):
        at = pl.multiple_of(offset_ref[0], 128)
        copy = pltpu.make_async_copy(cov_ref.at[:, pl.ds(at, rows)], corner, sem)
        copy.start()
        out_ref[:count, :] = dot2(snap_ref[...], basis_ref[...], lead)
        snap = snap_ref[...].astype(jnp.float32)
        energy = jnp.sum(jnp.sum(snap * snap, axis=1, keepdims=True), axis=0, keepdims=True)
        copy.wait()
        row_at = lax.broadcasted_iota(jnp.int32, (rows, rows), 0)
        col_at = lax.broadcasted_iota(jnp.int32, (rows, rows), 1)
        diagonal = jnp.where(row_at == col_at, corner[...], 0.0)
        trace = jnp.sum(jnp.sum(diagonal, axis=1, keepdims=True), axis=0, keepdims=True)
        share = forget_factor * trace + energy * (1.0 / count)
        out_ref[count:, :] = jnp.broadcast_to(share, (pad_rows, rank))

    return pl.pallas_call(
        kernel,
        out_shape=jax.ShapeDtypeStruct((count + pad_rows, rank), jnp.float32),
        in_specs=[in_smem, any_space, in_vmem, in_vmem],
        out_specs=in_vmem,
        scratch_shapes=[pltpu.VMEM((rows, rows), jnp.float32), pltpu.SemaphoreType.DMA],
        compiler_params=params,
        name="prepare",
    )(offset, prior_cov, snapshot_panel, basis)


def add_products(refs, offset_ref, cov_ref, block_refs, running, cov_bufs, block_bufs, sems):
    copies = []
    for at, (block_ref, cov_buf, block_buf) in enumerate(zip(block_refs, cov_bufs, block_bufs)):
        width = block_ref.shape[0]
        first = pl.multiple_of(offset_ref[at], 128)
        pair = (
            pltpu.make_async_copy(cov_ref.at[:, pl.ds(first, width)], cov_buf, sems.at[at, 0]),
            pltpu.make_async_copy(block_ref, block_buf, sems.at[at, 1]),
        )
        for copy in pair:
            copy.start()
        copies.append(pair)
    rank = block_refs[0].shape[1]
    for pair, cov_buf, block_buf in zip(copies, cov_bufs, block_bufs):
        for copy in pair:
            copy.wait()
        high, low = split(block_buf[...])
        both = jnp.concatenate([high, low], axis=1)
        cov_high, cov_low = split(cov_buf[...])
        wide = dot(cov_high, both, inner)
        running = running + (wide[:, :rank] + (wide[:, rank:] + dot(cov_low, high, inner)))
    return running


def product_scratch(rows, blocks):
    return (
        [pltpu.VMEM((rows, b.shape[0]), jnp.float32) for b in blocks]
        + [pltpu.VMEM(b.shape, jnp.float32) for b in blocks]
        + [pltpu.SemaphoreType.DMA((len(blocks), 2))]
    )


def product_part(offsets, prior_cov, blocks, running):
    rows, rank = prior_cov.shape[0], blocks[0].shape[1]
    count = len(blocks)
    more = [] if running is None else [running]

    def kernel(offset_ref, cov_ref, *refs):
        block_refs, refs = refs[:count], refs[count:]
        start = 0.0
        if more:
            start, refs = refs[0][...], refs[1:]
        out_ref, refs = refs[0], refs[1:]
        out_ref[...] = add_products(
            None, offset_ref, cov_ref, block_refs, start, refs[:count], refs[count:-1], refs[-1]
        )

    return pl.pallas_call(
        kernel,
        out_shape=jax.ShapeDtypeStruct((rows, rank), jnp.float32),
        in_specs=[in_smem, any_space] + [any_space] * count + [in_vmem] * len(more),
        out_specs=in_vmem,
        scratch_shapes=product_scratch(rows, blocks),
        compiler_params=params,
        name="product_part",
    )(offsets, prior_cov, *blocks, *more)


def product_end(offsets, prior_cov, blocks, running, totals, scale, snapshots, window, previous):
    rows, order = prior_cov.shape
    rank = blocks[0].shape[1]
    windows, _, snap_count = snapshots.shape
    count = len(blocks)
    last = window == windows - 1
    more = [] if previous is None else [previous]
    inv_snap = 1.0 / snap_count

    def kernel(offset_ref, cov_ref, *refs):
        block_refs, refs = refs[:count], refs[count:]
        running_ref, totals_ref, scale_ref, snap_ref = refs[:4]
        refs = refs[4:]
        if more:
            previous_ref, refs = refs[0], refs[1:]
        if last:
            applied_ref, part_ref = refs[:2]
            refs = refs[2:]
        else:
            scaled_ref, part_ref = refs[:2]
            refs = refs[2:]
        product = add_products(
            None,
            offset_ref,
            cov_ref,
            block_refs,
            running_ref[...],
            refs[:count],
            refs[count:-1],
            refs[-1],
        )
        applied = product * forget_factor ** (window + 1)
        for w in range(window + 1):
            total = totals_ref[w * snap_count : (w + 1) * snap_count, :]
            weight = forget_factor ** (window - w) * inv_snap
            applied = applied + weight * dot2(snap_ref[w], total, inner)
        factor = float(order) / jnp.sum(scale_ref[...][:1, :1], axis=0, keepdims=True)
        if more:
            applied = dot3(applied, previous_ref[...], trail) / factor
        gram = dot3(applied, applied, lead)
        if last:
            applied_ref[...] = applied
            part_ref[...] = gram
        else:
            scaled = applied * factor
            scaled_ref[...] = scaled
            part_ref[:rank, :] = gram
            for w in range(window + 2):
                at = rank + w * snap_count
                part_ref[at : at + snap_count, :] = dot2(snap_ref[w], scaled, lead)

    part_rows = rank if last else rank + (window + 2) * snap_count
    return pl.pallas_call(
        kernel,
        out_shape=(
            jax.ShapeDtypeStruct((rows, rank), jnp.float32),
            jax.ShapeDtypeStruct((part_rows, rank), jnp.float32),
        ),
        in_specs=[in_smem, any_space] + [any_space] * count + [in_vmem] * (4 + len(more)),
        out_specs=(in_vmem, in_vmem),
        scratch_shapes=product_scratch(rows, blocks),
        compiler_params=params,
        name="product_end",
    )(offsets, prior_cov, *blocks, running, totals, scale, snapshots, *more)


def inverse_factor(gram, rank):
    inverse = (
        lax.broadcasted_iota(jnp.int32, (rank, rank), 0)
        == lax.broadcasted_iota(jnp.int32, (rank, rank), 1)
    ).astype(jnp.float32)
    done = []
    for step in range(rank):
        at = step % 8
        root = lax.rsqrt(gram[at : at + 1, step : step + 1])
        row = gram[at : at + 1, :] * root
        inverse_row = inverse[at : at + 1, :] * root
        row_at = lax.broadcasted_iota(jnp.int32, (gram.shape[0], 1), 0)
        column = jnp.where(row_at > at, gram[:, step : step + 1] * root, 0.0)
        gram = gram - column * row
        inverse = jnp.where(row_at == at, inverse_row, inverse - column * inverse_row)
        if at == 7:
            done.append(inverse[:8])
            gram, inverse = gram[8:], inverse[8:]
    return jnp.concatenate(done, axis=0)


def factor_kernel(gram, applied):
    rank = gram.shape[1]
    more = [] if applied is None else [applied]

    def kernel(gram_ref, *refs):
        inverse = inverse_factor(gram_ref[:rank, :], rank)
        if more:
            inverse = dot3(refs[0][...], inverse, trail)
        refs[-1][...] = inverse

    return pl.pallas_call(
        kernel,
        out_shape=jax.ShapeDtypeStruct((applied if more else gram[:rank]).shape, jnp.float32),
        in_specs=[in_vmem] * (1 + len(more)),
        out_specs=in_vmem,
        compiler_params=params,
        name="factor",
    )(gram, *more)


def covariance_part(offsets, prior_cov, snapshots, blocks, filled):
    rows, _ = prior_cov.shape
    windows, _, snap_count = snapshots.shape
    count = len(blocks)
    more = [] if filled is None else [filled]
    inv_snap = 1.0 / snap_count

    def kernel(offset_ref, cov_ref, snap_ref, *refs):
        block_refs, refs = refs[:count], refs[count + len(more) :]
        out_ref, refs = refs[0], refs[1:]
        cov_bufs, block_bufs, out_bufs = refs[:count], refs[count : 2 * count], refs[2 * count : 3 * count]
        sems = refs[-1]
        copies = []
        for at in range(count):
            width = block_refs[at].shape[1]
            first = pl.multiple_of(offset_ref[at], 128)
            trio = (
                pltpu.make_async_copy(cov_ref.at[:, pl.ds(first, width)], cov_bufs[at], sems.at[at, 0]),
                pltpu.make_async_copy(block_refs[at], block_bufs[at], sems.at[at, 1]),
                pltpu.make_async_copy(out_bufs[at], out_ref.at[:, pl.ds(first, width)], sems.at[at, 2]),
            )
            trio[0].start()
            trio[1].start()
            copies.append(trio)
        for at in range(count):
            copies[at][0].wait()
            copies[at][1].wait()
            total = cov_bufs[at][...] * forget_factor**windows
            for w in range(windows):
                weight = forget_factor ** (windows - 1 - w) * inv_snap
                total = total + weight * dot(snap_ref[w], block_bufs[at][w], trail)
            out_bufs[at][...] = total
            copies[at][2].start()
        for at in range(count):
            copies[at][2].wait()

    widths = [b.shape[1] for b in blocks]
    return pl.pallas_call(
        kernel,
        out_shape=jax.ShapeDtypeStruct(prior_cov.shape, jnp.float32),
        in_specs=[in_smem, any_space, in_vmem] + [any_space] * (count + len(more)),
        out_specs=any_space,
        scratch_shapes=[pltpu.VMEM((rows, w), jnp.float32) for w in widths]
        + [pltpu.VMEM(b.shape, jnp.bfloat16) for b in blocks]
        + [pltpu.VMEM((rows, w), jnp.float32) for w in widths]
        + [pltpu.SemaphoreType.DMA((count, 3))],
        input_output_aliases={3 + count: 0} if more else {},
        compiler_params=params,
        name="covariance_part",
    )(offsets, prior_cov, snapshots, *blocks, *more)


def local(devices, prior_cov, snapshots, prior_basis):
    rows = prior_cov.shape[0]
    rank = prior_basis.shape[1]
    windows, _, snap_count = snapshots.shape
    groups = ring_offsets(devices, rows)
    offsets = jnp.stack([o for group in groups for o in group]).astype(jnp.int32)
    starts, at = [], 0
    for group in groups:
        starts.append(at)
        at += len(group)
    starts.append(at)

    def offsets_of(first, end):
        return lax.slice_in_dim(offsets, starts[first], starts[end])

    group_count = len(groups)
    bounds = [0, 2] + list(range(3, group_count - 1)) + [group_count]

    sent = prior_basis
    part = prepare(offsets, prior_cov, snapshots[0], prior_basis)
    sums = total_over_row(part, devices)
    scale, totals = sums[snap_count:], sums[:snap_count]
    inverse = None
    for window in range(windows):
        gathered = ring_gather(sent, devices, 0)
        running = None
        for first, end in zip(bounds[:-2], bounds[1:-1]):
            blocks = [b for group in gathered[first:end] for b in group]
            running = product_part(offsets_of(first, end), prior_cov, blocks, running)
        first, end = bounds[-2:]
        blocks = [b for group in gathered[first:end] for b in group]
        result, part = product_end(
            offsets_of(first, end),
            prior_cov,
            blocks,
            running,
            totals,
            scale,
            snapshots,
            window,
            inverse,
        )
        sums = total_over_row(part, devices)
        if window < windows - 1:
            sent = result
            totals = sums[rank:]
            inverse = factor_kernel(sums[:rank], None)
    new_basis = factor_kernel(sums, result)

    gathered = ring_gather(snapshots, devices, 1)
    new_cov = None
    for first, end in zip(bounds[:-1], bounds[1:]):
        blocks = [b for group in gathered[first:end] for b in group]
        new_cov = covariance_part(offsets_of(first, end), prior_cov, snapshots, blocks, new_cov)
    return (new_cov, new_basis)


def solution(mesh):
    return jax.shard_map(
        functools.partial(local, mesh.shape["row"]),
        mesh=mesh,
        in_specs=(
            P(("band", "row"), None),
            P(None, ("band", "row"), None),
            P(("band", "row"), None),
        ),
        out_specs=(P(("band", "row"), None), P(("band", "row"), None)),
        check_vma=False,
    )
```

```python
import functools

import jax
import jax.numpy as jnp
import numpy as np
from jax import lax
from jax.experimental import pallas as pl
from jax.experimental.pallas import tpu as pltpu
from jax.sharding import PartitionSpec as P

forget_factor = 0.9
code_span = 240.0
code_middle = 120.0
scale_rows = 16
ln2 = 0.6931471805599453
in_vmem = pl.BlockSpec(memory_space=pltpu.VMEM)
anywhere = pl.BlockSpec(memory_space=pl.ANY)
in_hbm = pl.BlockSpec(memory_space=pltpu.HBM)
in_smem = pl.BlockSpec(memory_space=pltpu.SMEM)
params = pltpu.CompilerParams(vmem_limit_bytes=16 * 2**20)

inner = (((1,), (0,)), ((), ()))
lead = (((0,), (0,)), ((), ()))
trail = (((1,), (1,)), ((), ()))


def dot(a, b, dims):
    return lax.dot_general(a, b, dims, preferred_element_type=jnp.float32)


def split(x):
    high = x.astype(jnp.bfloat16)
    return high, (x - high.astype(jnp.float32)).astype(jnp.bfloat16)


def dot3(a, b, dims):
    a_high, a_low = split(a)
    b_high, b_low = split(b)
    return dot(a_high, b_high, dims) + (dot(a_high, b_low, dims) + dot(a_low, b_high, dims))


def dot2(a, b, dims):
    b_high, b_low = split(b)
    return dot(a, b_high, dims) + dot(a, b_low, dims)


def gate(values, events=()):
    count = len(values)

    def kernel(*refs):
        pass

    return list(
        pl.pallas_call(
            kernel,
            out_shape=tuple(jax.ShapeDtypeStruct(v.shape, v.dtype) for v in values),
            in_specs=[anywhere] * (count + len(events)),
            out_specs=(anywhere,) * count,
            input_output_aliases={i: i for i in range(count)},
            compiler_params=params,
            name="gate",
        )(*values, *events)
    )


def ring_order(devices):
    chips = devices // 2
    return list(range(0, chips, 2)) + list(range(chips - 1, 0, -2))


def ring_pairs(devices, way):
    order = ring_order(devices)
    chips = len(order)
    pairs = []
    for at in range(chips):
        for core in range(2):
            pairs.append((2 * order[at] + core, 2 * order[(at + way) % chips] + core))
    return pairs


def partner_pairs(devices, mask):
    return [(i, i ^ mask) for i in range(devices)]


def ring_table(devices, rows):
    order = ring_order(devices)
    chips = len(order)
    table = []
    for me in range(devices):
        at, core = order.index(me // 2), me % 2
        line = [me * rows, (me ^ 1) * rows]
        for step in range(1, chips // 2):
            for there in (at - step, at + step):
                chip = order[there % chips]
                line += [(2 * chip + core) * rows, (2 * chip + 1 - core) * rows]
        chip = order[(at + chips // 2) % chips]
        own, other = (2 * chip + core) * rows, (2 * chip + 1 - core) * rows
        line += [own, other, own + rows // 2, other + rows // 2]
        line += [core, (me // 2) % 2]
        table.append(line)
    return np.array(table, np.int32)


class Ring:
    def __init__(self, block, devices, axis):
        self.axis = axis
        self.forth, self.back = ring_pairs(devices, 1), ring_pairs(devices, -1)
        self.swap = partner_pairs(devices, 1)
        self.steps = devices // 4
        self.done = 0
        self.ahead = self.behind = block
        self.groups = []

    def pass_on(self):
        mine = [self.ahead] if self.done == 0 else [self.ahead, self.behind]
        group = []
        for block in mine:
            group += [block, lax.ppermute(block, "row", self.swap)]
        self.groups.append(group)

    def step(self):
        self.done += 1
        ahead, behind = self.ahead, self.behind
        if self.done == self.steps:
            half = ahead.shape[self.axis] // 2
            ahead = lax.slice_in_dim(ahead, 0, half, axis=self.axis)
            behind = lax.slice_in_dim(behind, half, 2 * half, axis=self.axis)
        self.ahead = lax.ppermute(ahead, "row", self.forth)
        self.behind = lax.ppermute(behind, "row", self.back)

    def held(self):
        received = [self.groups[-1][1::2]] if self.groups else []
        return [self.ahead, self.behind] + [v for r in received for v in r]

    def hold(self, values):
        values = list(values)
        self.ahead, self.behind = values[:2]
        if self.groups:
            self.groups[-1][1::2] = values[2:]


def small_kernel(kernel, out_shape, args, name):
    multiple = isinstance(out_shape, tuple)
    return pl.pallas_call(
        kernel,
        out_shape=out_shape,
        in_specs=[in_smem] + [in_vmem] * (len(args) - 1),
        out_specs=tuple(in_vmem for _ in out_shape) if multiple else in_vmem,
        compiler_params=params,
        name=name,
    )(*args)


def f32(*shape):
    return jax.ShapeDtypeStruct(shape, jnp.float32)


def store_halves(line_ref, bit, value_ref, mine_ref, theirs_ref):
    half = mine_ref.shape[0]
    side = line_ref[0, bit]
    mine_ref[...] = value_ref[pl.ds(pl.multiple_of(side * half, 8), half), :]
    theirs_ref[...] = value_ref[pl.ds(pl.multiple_of((1 - side) * half, 8), half), :]


def add_two(line, a, b):
    def kernel(line_ref, a_ref, b_ref, out_ref):
        out_ref[...] = a_ref[...] + b_ref[...]

    return small_kernel(kernel, f32(*a.shape), (line, a, b), "add_two")


def add_and_halve(line, bit, a, b):
    half = f32(a.shape[0] // 2, a.shape[1])

    def kernel(line_ref, a_ref, b_ref, mine_ref, theirs_ref):
        size = mine_ref.shape[0]
        side = line_ref[0, bit]
        for out_ref, which in ((mine_ref, side), (theirs_ref, 1 - side)):
            rows = pl.ds(pl.multiple_of(which * size, 8), size)
            out_ref[...] = a_ref[rows, :] + b_ref[rows, :]

    return small_kernel(kernel, (half, half), (line, a, b), "add_and_halve")


def join_halves(line, bit, mine, theirs):
    def kernel(line_ref, mine_ref, theirs_ref, out_ref):
        size = mine_ref.shape[0]
        side = line_ref[0, bit]
        out_ref[pl.ds(pl.multiple_of(side * size, 8), size), :] = mine_ref[...]
        out_ref[pl.ds(pl.multiple_of((1 - side) * size, 8), size), :] = theirs_ref[...]

    shape = f32(2 * mine.shape[0], mine.shape[1])
    return small_kernel(kernel, shape, (line, mine, theirs), "join_halves")


class Total:
    def __init__(self, line, bits, mine, theirs, devices, halve_chips):
        self.line, self.bits, self.devices = line, bits, devices
        self.mine, self.theirs = mine, theirs
        first = 4 if halve_chips else 2
        self.rounds = ["core"] + ["halve"] * halve_chips
        while first < devices:
            self.rounds.append(first)
            first *= 2
        self.rounds += ["join"] * halve_chips + ["last"]

    def pass_on(self, value, mask):
        return lax.ppermute(value, "row", partner_pairs(self.devices, mask))

    def round(self, count=1):
        for _ in range(count):
            if not self.rounds:
                return
            kind = self.rounds.pop(0)
            line, (core_bit, chip_bit) = self.line, self.bits
            if kind == "core":
                got = self.pass_on(self.theirs, 1)
                if self.rounds[0] == "halve":
                    self.mine, self.theirs = add_and_halve(line, chip_bit, self.mine, got)
                else:
                    self.mine, self.theirs = add_two(line, self.mine, got), None
            elif kind == "halve":
                self.mine = add_two(line, self.mine, self.pass_on(self.theirs, 2))
                self.theirs = None
            elif kind == "join":
                self.mine = join_halves(line, chip_bit, self.mine, self.pass_on(self.mine, 2))
            elif kind == "last":
                self.mine = join_halves(line, core_bit, self.mine, self.pass_on(self.mine, 1))
            else:
                self.mine = add_two(line, self.mine, self.pass_on(self.mine, kind))

    def held(self):
        return [self.mine] if self.theirs is None else [self.mine, self.theirs]

    def hold(self, values):
        self.mine = values[0]
        if self.theirs is not None:
            self.theirs = values[1]


def gate_all(parts, extra=(), events=()):
    lists = [p.held() for p in parts]
    flat = [v for values in lists for v in values] + list(extra)
    flat = gate(flat, events)
    at = 0
    for p, values in zip(parts, lists):
        p.hold(flat[at : at + len(values)])
        at += len(values)
    return flat[at:]


def encode(values):
    size = jnp.abs(values)
    most = jnp.max(size, axis=0, keepdims=True)
    level = size / jnp.maximum(most, 1e-37)
    power = jnp.exp((level * code_span - code_middle) * ln2)
    return jnp.where(values < 0.0, -power, power).astype(jnp.bfloat16), most


def decode(code, most):
    code = code.astype(jnp.float32)
    level = (jnp.log(jnp.abs(code)) * (1.0 / ln2) + code_middle) * (1.0 / code_span)
    return jnp.where(code < 0.0, -level, level) * most


def write_rows(rows):
    at = lax.broadcasted_iota(jnp.int32, (scale_rows, rows[0].shape[1]), 0)
    block = jnp.zeros(at.shape, jnp.float32)
    for i, row in enumerate(rows):
        high = row.astype(jnp.bfloat16).astype(jnp.float32)
        block = jnp.where(at == 2 * i, high, block)
        block = jnp.where(at == 2 * i + 1, row - high, block)
    return block.astype(jnp.bfloat16)


def read_row(block, i):
    block = block.astype(jnp.float32)
    return block[2 * i : 2 * i + 1] + block[2 * i + 1 : 2 * i + 2]


def pack(line, values, mine, got, extra):
    rows, rank = values.shape
    sum_rows = mine.shape[0]
    half, sum_half = rows // 2, sum_rows // 2
    size = half + scale_rows + sum_half
    more = [] if extra is None else [extra]

    def kernel(line_ref, values_ref, mine_ref, got_ref, *refs):
        out_ref = refs[-1]
        sums = mine_ref[...] + got_ref[...]
        for h in range(2):
            code, most = encode(values_ref[h * half : (h + 1) * half, :])
            sum_code, sum_most = encode(sums[h * sum_half : (h + 1) * sum_half])
            scales = [most, sum_most]
            if more:
                scales += [refs[0][w : w + 1, :] for w in range(2)]
            at = h * size
            out_ref[at : at + half, :] = code
            out_ref[at + half : at + half + scale_rows, :] = write_rows(scales)
            out_ref[at + half + scale_rows : at + size, :] = sum_code

    return small_kernel(
        kernel,
        jax.ShapeDtypeStruct((2 * size, rank), jnp.bfloat16),
        (line, values, mine, got, *more),
        "pack",
    )


def prepare(line, bits, prior_cov, snapshots, basis):
    windows, rows, count = snapshots.shape
    rank = basis.shape[1]
    pieces = rows // 128
    half = f32(count // 2, rank)

    def total(x):
        return jnp.sum(jnp.sum(x, axis=0, keepdims=True), axis=1, keepdims=True)

    def kernel(line_ref, cov_ref, snap_ref, basis_ref, mine_ref, theirs_ref, share_ref, corner, part, sem):
        copies = []
        for at in range(pieces):
            first = pl.multiple_of(line_ref[0, 0] + at * 128, 128)
            copies.append(
                pltpu.make_async_copy(
                    cov_ref.at[pl.ds(at * 128, 128), pl.ds(first, 128)], corner.at[at], sem.at[at]
                )
            )
        for copy in copies:
            copy.start()
        part[...] = dot2(snap_ref[0], basis_ref[...], lead)
        store_halves(line_ref, bits[0], part, mine_ref, theirs_ref)
        energies = []
        for w in range(windows):
            snap = snap_ref[w].astype(jnp.float32)
            energies.append(total(snap * snap) * (1.0 / count))
        row_at = lax.broadcasted_iota(jnp.int32, (128, 128), 0)
        col_at = lax.broadcasted_iota(jnp.int32, (128, 128), 1)
        diagonal = jnp.zeros((128, 128), jnp.float32)
        for at in range(pieces):
            copies[at].wait()
            diagonal = diagonal + jnp.where(row_at == col_at, corner[at], 0.0)
        trace = total(diagonal)
        for w in range(windows):
            trace = forget_factor * trace + energies[w]
            share_ref[w : w + 1, :] = jnp.broadcast_to(trace, (1, rank))
        share_ref[windows:, :] = jnp.zeros((8 - windows, rank), jnp.float32)

    return pl.pallas_call(
        kernel,
        out_shape=(half, half, f32(8, rank)),
        in_specs=[in_smem, anywhere, in_vmem, in_vmem],
        out_specs=(in_vmem, in_vmem, in_vmem),
        scratch_shapes=[
            pltpu.VMEM((pieces, 128, 128), jnp.float32),
            pltpu.VMEM((count, rank), jnp.float32),
            pltpu.SemaphoreType.DMA((pieces,)),
        ],
        compiler_params=pltpu.CompilerParams(vmem_limit_bytes=50 * 2**20),
        name="prepare",
    )(line, prior_cov, snapshots, basis)


def add_products(line_ref, base, cov_ref, block_refs, state, first_window):
    running, own, other, misc, gram = state
    rows = cov_ref.shape[0]
    rank = running.shape[1]
    half = rows // 2
    sum_half = own.shape[0] // 2
    size = half + scale_rows + sum_half
    for at, block_ref in enumerate(block_refs):
        whole = block_ref.shape[0] == 2 * size
        first = pl.multiple_of(line_ref[0, base + at], 128)
        pieces, sums = [], []
        for h in (0, 1) if whole else (at // 2,):
            start = h * size if whole else 0
            scales = block_ref[start + half : start + half + scale_rows, :]
            most = read_row(scales, 0)
            pieces.append(decode(block_ref[start : start + half, :], most))
            coded = block_ref[start + half + scale_rows : start + size, :]
            sums.append(decode(coded, read_row(scales, 1)))
            if first_window:
                peak = jnp.maximum(misc[2:3], most)
                traces = [misc[w : w + 1] for w in range(2)]
                if h == 0:
                    traces = [t + read_row(scales, 2 + w) for w, t in enumerate(traces)]
                misc = jnp.concatenate(traces + [peak, misc[3:]], axis=0)
        block = jnp.concatenate(pieces, axis=0) if whole else pieces[0]
        if whole:
            piece = jnp.concatenate(sums, axis=0)
        else:
            nothing = jnp.zeros((sum_half, rank), jnp.float32)
            piece = jnp.concatenate(
                [sums[0], nothing] if at // 2 == 0 else [nothing, sums[0]], axis=0
            )
        if at % 2 == 0:
            own = own + piece
        else:
            other = other + piece
        high, low = split(block)
        both = jnp.concatenate([high, low], axis=1)
        cov_high, cov_low = split(cov_ref[:, pl.ds(first, block.shape[0])])
        wide = dot(cov_high, both, inner)
        running = running + (wide[:, :rank] + (wide[:, rank:] + dot(cov_low, high, inner)))
        if gram is not None:
            square = dot(high, both, lead)
            gram = gram + (square[:, :rank] + (square[:, rank:] + dot(low, high, lead)))
    return running, own, other, misc, gram


def empty_state(rows, rank, sum_rows, first_window):
    state = [jnp.zeros((n, rank), jnp.float32) for n in (rows, sum_rows, sum_rows, 8)]
    return state + [None if first_window else jnp.zeros((rank, rank), jnp.float32)]


def product_part(line, base, prior_cov, blocks, state, sum_rows, first_window):
    count = len(blocks)
    rows, rank = prior_cov.shape[0], blocks[0].shape[1]
    shapes = [f32(n, rank) for n in (rows, sum_rows, sum_rows, 8)]
    if not first_window:
        shapes.append(f32(rank, rank))
    outs = len(shapes)
    more = [] if state is None else list(state)

    def kernel(line_ref, cov_ref, *refs):
        old = empty_state(rows, rank, sum_rows, first_window)
        for i in range(len(more)):
            old[i] = refs[count + i][...]
        new = add_products(line_ref, base, cov_ref, refs[:count], old, first_window)
        for out_ref, value in zip(refs[-outs:], new):
            out_ref[...] = value

    return list(
        small_kernel(kernel, tuple(shapes), (line, prior_cov, *blocks, *more), "product_part")
    )


def product_end(line, bits, base, prior_cov, blocks, state, misc, snapshots, window):
    rows, order = prior_cov.shape
    rank = blocks[0].shape[1]
    windows, _, snap_count = snapshots.shape
    count = len(blocks)
    last = window == windows - 1
    first_window = window == 0
    sum_rows = state[1].shape[0]
    inv_snap = 1.0 / snap_count
    parts = len(state)
    more = [] if misc is None else [misc]
    if last:
        shapes = (f32(rows, rank), f32(rank // 2, rank), f32(rank // 2, rank), f32(rank, rank))
    else:
        shapes = (f32(rows, rank), f32(8, rank))

    def kernel(line_ref, cov_ref, *refs):
        block_refs, refs = refs[:count], refs[count:]
        old = [r[...] for r in refs[:parts]] + [None] * (5 - parts)
        snap_ref, refs = refs[parts], refs[parts + 1 :]
        if more:
            misc_ref, refs = refs[0], refs[1:]
        outs, sums_buf, gram_buf = refs[: len(shapes)], refs[-2], refs[-1]
        product, own, other, new_misc, gram = add_products(
            line_ref, base, cov_ref, block_refs, old, first_window
        )
        side = line_ref[0, bits[0]]
        sums_buf[pl.ds(pl.multiple_of(side * sum_rows, 8), sum_rows), :] = own
        sums_buf[pl.ds(pl.multiple_of((1 - side) * sum_rows, 8), sum_rows), :] = other
        applied = product * forget_factor ** (window + 1)
        for w in range(window + 1):
            at = w * snap_count
            weight = forget_factor ** (window - w) * inv_snap
            applied = applied + weight * dot2(
                snap_ref[w], sums_buf[at : at + snap_count, :], inner
            )
        if more:
            new_misc = misc_ref[...]
        factor = float(order) / new_misc[window : window + 1]
        if first_window:
            factor = factor / jnp.maximum(new_misc[2:3], 1e-37)
        applied = applied * factor
        outs[0][...] = applied
        if last:
            gram_buf[...] = lax.dot_general(
                applied,
                applied,
                lead,
                precision=lax.Precision.HIGHEST,
                preferred_element_type=jnp.float32,
            )
            store_halves(line_ref, bits[0], gram_buf, outs[1], outs[2])
            outs[3][...] = gram
        else:
            outs[1][...] = new_misc

    return pl.pallas_call(
        kernel,
        out_shape=shapes,
        in_specs=[in_smem] + [in_vmem] * (2 + count + parts + len(more)),
        out_specs=tuple(in_vmem for _ in shapes),
        scratch_shapes=[
            pltpu.VMEM((2 * sum_rows, rank), jnp.float32),
            pltpu.VMEM((rank, rank), jnp.float32),
        ],
        compiler_params=params,
        name="product_end",
    )(line, prior_cov, *blocks, *state, snapshots, *more)


def window_sums(line, bits, applied, snapshots):
    windows, _, snap_count = snapshots.shape
    rank = applied.shape[1]
    total = windows * snap_count
    half = f32(total // 2, rank)

    def kernel(line_ref, applied_ref, snap_ref, mine_ref, theirs_ref, part):
        for w in range(windows):
            at = w * snap_count
            part[at : at + snap_count, :] = dot2(snap_ref[w], applied_ref[...], lead)
        store_halves(line_ref, bits[0], part, mine_ref, theirs_ref)

    return pl.pallas_call(
        kernel,
        out_shape=(half, half),
        in_specs=[in_smem] + [in_vmem] * 2,
        out_specs=(in_vmem, in_vmem),
        scratch_shapes=[pltpu.VMEM((total, rank), jnp.float32)],
        compiler_params=params,
        name="window_sums",
    )(line, applied, snapshots)


panel = 8


def factor_panel(gram, inverse, first):
    rank = gram.shape[1]
    sub = lax.broadcasted_iota(jnp.int32, (panel, rank), 0)
    top, top_inverse = gram[:panel], inverse[:panel]
    columns = [
        jnp.broadcast_to(top[:, first + k : first + k + 1], (panel, rank)) for k in range(panel)
    ]
    roots = jnp.zeros((panel, rank), jnp.float32)
    for k in range(panel):
        root = lax.rsqrt(columns[k][k : k + 1])
        roots = jnp.where(sub == k, root, roots)
        scaled = jnp.where(sub > k, columns[k] * (root * root), 0.0)
        top = top - scaled * top[k : k + 1]
        top_inverse = top_inverse - scaled * top_inverse[k : k + 1]
        for m in range(k + 1, panel):
            columns[m] = columns[m] - scaled * columns[m][k : k + 1]
    top, top_inverse = top * roots, top_inverse * roots
    rest, rest_inverse = gram[panel:], inverse[panel:]
    if rest.shape[0]:
        change = lax.dot_general(
            top,
            jnp.concatenate([top, top_inverse], axis=1),
            lead,
            precision=lax.Precision.HIGHEST,
            preferred_element_type=jnp.float32,
        )[first + panel :]
        rest = rest - change[:, :rank]
        rest_inverse = rest_inverse - change[:, rank:]
    return top_inverse, rest, rest_inverse


def factor_rows(gram, inverse, first, end):
    done = []
    for at in range(first, end, panel):
        rows, gram, inverse = factor_panel(gram, inverse, at)
        done.append(rows)
    return jnp.concatenate(done, axis=0), gram, inverse


def identity(rank):
    return (
        lax.broadcasted_iota(jnp.int32, (rank, rank), 0)
        == lax.broadcasted_iota(jnp.int32, (rank, rank), 1)
    ).astype(jnp.float32)


def factor_some(line, state, first, end):
    rank = state[0].shape[1]
    left = rank - end
    begin = len(state) == 1
    shapes = (f32(end - first, rank),) + ((f32(left, rank),) * 2 if left else ())

    def kernel(line_ref, *refs):
        inverse = identity(rank) if begin else refs[1][...]
        new = factor_rows(refs[0][...], inverse, first, end)
        for out_ref, value in zip(refs[len(state) :], new):
            out_ref[...] = value

    return list(small_kernel(kernel, shapes, (line, *state), "factor_some"))


def finish(line, bits, gram, theirs, previous, applied):
    rank = applied.shape[1]
    half = rank // 2

    def kernel(line_ref, gram_ref, theirs_ref, *refs):
        applied_ref, out_ref, buf = refs[-3:]
        side = line_ref[0, bits[0]]
        buf[pl.ds(pl.multiple_of(side * half, 8), half), :] = gram_ref[...]
        buf[pl.ds(pl.multiple_of((1 - side) * half, 8), half), :] = theirs_ref[...]
        first = jnp.concatenate([r[...] for r in refs[:-3]], axis=0)

        def exact(a, b, dims):
            return lax.dot_general(
                a,
                b,
                dims,
                precision=lax.Precision.HIGHEST,
                preferred_element_type=jnp.float32,
            )

        second_gram = exact(exact(first, buf[...], inner), first, trail)
        second, _, _ = factor_rows(second_gram, identity(rank), 0, rank)
        out_ref[...] = dot3(applied_ref[...], exact(second, first, inner), trail)

    return pl.pallas_call(
        kernel,
        out_shape=f32(*applied.shape),
        in_specs=[in_smem] + [in_vmem] * (3 + len(previous)),
        out_specs=in_vmem,
        scratch_shapes=[pltpu.VMEM((rank, rank), jnp.float32)],
        compiler_params=params,
        name="finish",
    )(line, gram, theirs, *previous, applied)


def covariance_part(line, base, prior_cov, snapshots, blocks, filled):
    rows, _ = prior_cov.shape
    windows, _, snap_count = snapshots.shape
    count = len(blocks)
    more = [] if filled is None else [filled]
    inv_snap = 1.0 / snap_count

    def kernel(line_ref, cov_ref, snap_ref, *refs):
        block_refs, refs = refs[:count], refs[count + len(more) :]
        out_ref, out_bufs, sems = refs[0], refs[1:-1], refs[-1]
        copies = []
        for at in range(count):
            width = block_refs[at].shape[1]
            first = pl.multiple_of(line_ref[0, base + at], 128)
            columns = pl.ds(first, width)
            total = cov_ref[:, columns] * forget_factor**windows
            for w in range(windows):
                weight = forget_factor ** (windows - 1 - w) * inv_snap
                total = total + weight * dot(snap_ref[w], block_refs[at][w], trail)
            out_bufs[at][...] = total
            copy = pltpu.make_async_copy(out_bufs[at], out_ref.at[:, columns], sems.at[at])
            copy.start()
            copies.append(copy)
        for copy in copies:
            copy.wait()

    return pl.pallas_call(
        kernel,
        out_shape=f32(*prior_cov.shape),
        in_specs=[in_smem] + [in_vmem] * (2 + count) + [in_hbm] * len(more),
        out_specs=in_hbm,
        scratch_shapes=[pltpu.VMEM((rows, b.shape[1]), jnp.float32) for b in blocks]
        + [pltpu.SemaphoreType.DMA((count,))],
        input_output_aliases={3 + count: 0} if more else {},
        compiler_params=params,
        name="covariance_part",
    )(line, prior_cov, snapshots, *blocks, *more)


def local(devices, prior_cov, snapshots, prior_basis):
    rows = prior_cov.shape[0]
    rank = prior_basis.shape[1]
    windows, _, snap_count = snapshots.shape
    table = ring_table(devices, rows)
    me = lax.axis_index("row")
    line = lax.dynamic_slice_in_dim(jnp.asarray(table), me, 1, axis=0)
    entries = table.shape[1]
    bits = (entries - 2, entries - 1)
    steps = devices // 4
    starts = [0] + [2 + 4 * at for at in range(steps)]
    swap = partner_pairs(devices, 1)
    snap_ring = Ring(snapshots, devices, 1)

    def fill(filled, first, end):
        blocks = [b for group in snap_ring.groups[first:end] for b in group]
        return covariance_part(line, starts[first], prior_cov, snapshots, blocks, filled)

    mine, theirs, share = prepare(line, bits, prior_cov, snapshots, prior_basis)
    values, misc = prior_basis, None
    for window in range(windows):
        first_window = window == 0
        got = lax.ppermute(theirs, "row", swap)
        ring = Ring(pack(line, values, mine, got, share if first_window else None), devices, 0)
        sum_rows = mine.shape[0]
        state = None
        for phase in range(1, steps + 1):
            ring.pass_on()
            ring.step()
            if phase >= 2:
                group = phase - 2
                state = product_part(
                    line,
                    starts[group],
                    prior_cov,
                    ring.groups[group],
                    state,
                    sum_rows,
                    first_window,
                )
            collect = not first_window and phase == 2
            state = gate_all([ring, snap_ring] if collect else [ring], state or []) or None
            if collect:
                snap_ring.pass_on()
                snap_ring.step()
        ring.pass_on()
        if first_window:
            snap_ring.ahead = snap_ring.behind = gate([snapshots], [ring.ahead])[0]
            snap_ring.pass_on()
            snap_ring.step()
        state = product_part(
            line,
            starts[steps - 1],
            prior_cov,
            ring.groups[steps - 1],
            state,
            sum_rows,
            first_window,
        )
        result = product_end(
            line,
            bits,
            starts[steps],
            prior_cov,
            ring.groups[steps],
            state,
            misc,
            snapshots,
            window,
        )
        if first_window:
            values, misc = result
            mine, theirs = window_sums(line, bits, values, snapshots)
    applied, mine, theirs, first_gram = result
    total = Total(line, bits, mine, theirs, devices, False)
    total.rounds.pop()
    pieces, left = [], [first_gram]
    count = len(total.rounds)
    at = 0
    while total.rounds:
        total.round()
        end = rank if not total.rounds else min(rank, at + rank // (panel * count) * panel)
        done, *left = factor_some(line, left, at, end)
        pieces.append(done)
        at = end
        (pieces[-1], *left) = gate_all([total], [pieces[-1]] + left)
    new_cov = fill(None, 0, 2)
    theirs = lax.ppermute(total.mine, "row", swap)
    while snap_ring.done < steps:
        snap_ring.pass_on()
        snap_ring.step()
    new_basis = finish(line, bits, total.mine, theirs, pieces, applied)
    snap_ring.pass_on()
    for at in range(2, steps + 1):
        new_cov = fill(new_cov, at, at + 1)
    return (new_cov, new_basis)


def solution(mesh):
    return jax.shard_map(
        functools.partial(local, mesh.shape["row"]),
        mesh=mesh,
        in_specs=(
            P(("band", "row"), None),
            P(None, ("band", "row"), None),
            P(("band", "row"), None),
        ),
        out_specs=(P(("band", "row"), None), P(("band", "row"), None)),
        check_vma=False,
    )
```

```python
import functools

import jax
import jax.numpy as jnp
import numpy as np
from jax import lax
from jax.experimental import pallas as pl
from jax.experimental.pallas import tpu as pltpu
from jax.sharding import PartitionSpec as P

forget_factor = 0.9
code_span = 240.0
code_middle = 120.0
scale_rows = 16
ln2 = 0.6931471805599453
in_vmem = pl.BlockSpec(memory_space=pltpu.VMEM)
anywhere = pl.BlockSpec(memory_space=pl.ANY)
in_hbm = pl.BlockSpec(memory_space=pltpu.HBM)
in_smem = pl.BlockSpec(memory_space=pltpu.SMEM)
params = pltpu.CompilerParams(vmem_limit_bytes=16 * 2**20)

inner = (((1,), (0,)), ((), ()))
lead = (((0,), (0,)), ((), ()))
trail = (((1,), (1,)), ((), ()))


def dot(a, b, dims):
    return lax.dot_general(a, b, dims, preferred_element_type=jnp.float32)


def split(x):
    high = x.astype(jnp.bfloat16)
    return high, (x - high.astype(jnp.float32)).astype(jnp.bfloat16)


def dot3(a, b, dims):
    a_high, a_low = split(a)
    b_high, b_low = split(b)
    return dot(a_high, b_high, dims) + (dot(a_high, b_low, dims) + dot(a_low, b_high, dims))


def dot2(a, b, dims):
    b_high, b_low = split(b)
    return dot(a, b_high, dims) + dot(a, b_low, dims)


def gate(values, events=()):
    count = len(values)

    def kernel(*refs):
        pass

    return list(
        pl.pallas_call(
            kernel,
            out_shape=tuple(jax.ShapeDtypeStruct(v.shape, v.dtype) for v in values),
            in_specs=[anywhere] * (count + len(events)),
            out_specs=(anywhere,) * count,
            input_output_aliases={i: i for i in range(count)},
            compiler_params=params,
            name="gate",
        )(*values, *events)
    )


def ring_order(devices):
    chips = devices // 2
    return list(range(0, chips, 2)) + list(range(chips - 1, 0, -2))


def ring_pairs(devices, way):
    order = ring_order(devices)
    chips = len(order)
    pairs = []
    for at in range(chips):
        for core in range(2):
            pairs.append((2 * order[at] + core, 2 * order[(at + way) % chips] + core))
    return pairs


def partner_pairs(devices, mask):
    return [(i, i ^ mask) for i in range(devices)]


def ring_table(devices, rows):
    order = ring_order(devices)
    chips = len(order)
    table = []
    for me in range(devices):
        at, core = order.index(me // 2), me % 2
        line = [me * rows, (me ^ 1) * rows]
        for step in range(1, chips // 2):
            for there in (at - step, at + step):
                chip = order[there % chips]
                line += [(2 * chip + core) * rows, (2 * chip + 1 - core) * rows]
        chip = order[(at + chips // 2) % chips]
        line += [(2 * chip + core) * rows, (2 * chip + 1 - core) * rows]
        line += [core, (me // 2) % 2]
        table.append(line)
    return np.array(table, np.int32)


class Ring:
    def __init__(self, line, bits, block, devices):
        self.line, self.bits = line, bits
        self.forth, self.back = ring_pairs(devices, 1), ring_pairs(devices, -1)
        self.apart = [p for p in self.forth if p[0] % 2 == 0] + [
            p for p in self.back if p[0] % 2 == 1
        ]
        self.swap = partner_pairs(devices, 1)
        self.steps = devices // 4
        self.done = 0
        self.recent = [block]
        self.groups = []
        self.new_recent = self.new_swapped = False

    def pass_on(self, copies=None):
        group = []
        for block, copy in zip(self.recent, copies or self.recent):
            group += [block, lax.ppermute(copy, "row", self.swap)]
        self.groups.append(group)
        self.new_swapped = True

    def step(self):
        self.done += 1
        self.new_recent = True
        ahead, behind = self.recent[0], self.recent[-1]
        self.full = self.recent
        if self.done == self.steps:
            block = ahead
            if len(self.recent) == 2:
                block = choose(self.line, self.bits[0], ahead, behind)
            self.recent = [lax.ppermute(block, "row", self.apart)]
        else:
            self.recent = [
                lax.ppermute(ahead, "row", self.forth),
                lax.ppermute(behind, "row", self.back),
            ]

    def held(self):
        return (self.recent if self.new_recent else []) + (
            self.groups[-1][1::2] if self.new_swapped else []
        )

    def hold(self, values):
        values = list(values)
        if self.new_recent:
            old, count = self.recent, len(self.recent)
            self.recent, values = values[:count], values[count:]
            for group in self.groups:
                for at, block in enumerate(group):
                    for before, now in zip(old, self.recent):
                        if block is before:
                            group[at] = now
        if self.new_swapped:
            self.groups[-1][1::2] = values
        self.new_recent = self.new_swapped = False


def small_kernel(kernel, out_shape, args, name):
    multiple = isinstance(out_shape, tuple)
    return pl.pallas_call(
        kernel,
        out_shape=out_shape,
        in_specs=[in_smem] + [in_vmem] * (len(args) - 1),
        out_specs=tuple(in_vmem for _ in out_shape) if multiple else in_vmem,
        compiler_params=params,
        name=name,
    )(*args)


def f32(*shape):
    return jax.ShapeDtypeStruct(shape, jnp.float32)


def choose(line, bit, first, second):
    def kernel(line_ref, first_ref, second_ref, out_ref):
        @pl.when(line_ref[0, bit] == 0)
        def _():
            out_ref[...] = first_ref[...]

        @pl.when(line_ref[0, bit] == 1)
        def _():
            out_ref[...] = second_ref[...]

    shape = jax.ShapeDtypeStruct(first.shape, first.dtype)
    return small_kernel(kernel, shape, (line, first, second), "choose")


def store_halves(line_ref, bit, value_ref, mine_ref, theirs_ref):
    half = mine_ref.shape[0]
    side = line_ref[0, bit]
    mine_ref[...] = value_ref[pl.ds(pl.multiple_of(side * half, 8), half), :]
    theirs_ref[...] = value_ref[pl.ds(pl.multiple_of((1 - side) * half, 8), half), :]


def add_two(line, a, b):
    def kernel(line_ref, a_ref, b_ref, out_ref):
        out_ref[...] = a_ref[...] + b_ref[...]

    return small_kernel(kernel, f32(*a.shape), (line, a, b), "add_two")


def add_and_halve(line, bit, a, b):
    half = f32(a.shape[0] // 2, a.shape[1])

    def kernel(line_ref, a_ref, b_ref, mine_ref, theirs_ref):
        size = mine_ref.shape[0]
        side = line_ref[0, bit]
        for out_ref, which in ((mine_ref, side), (theirs_ref, 1 - side)):
            rows = pl.ds(pl.multiple_of(which * size, 8), size)
            out_ref[...] = a_ref[rows, :] + b_ref[rows, :]

    return small_kernel(kernel, (half, half), (line, a, b), "add_and_halve")


def join_halves(line, bit, mine, theirs):
    def kernel(line_ref, mine_ref, theirs_ref, out_ref):
        size = mine_ref.shape[0]
        side = line_ref[0, bit]
        out_ref[pl.ds(pl.multiple_of(side * size, 8), size), :] = mine_ref[...]
        out_ref[pl.ds(pl.multiple_of((1 - side) * size, 8), size), :] = theirs_ref[...]

    shape = f32(2 * mine.shape[0], mine.shape[1])
    return small_kernel(kernel, shape, (line, mine, theirs), "join_halves")


class Total:
    def __init__(self, line, bits, mine, theirs, devices, halve_chips):
        self.line, self.bits, self.devices = line, bits, devices
        self.mine, self.theirs = mine, theirs
        first = 4 if halve_chips else 2
        self.rounds = ["core"] + ["halve"] * halve_chips
        while first < devices:
            self.rounds.append(first)
            first *= 2
        self.rounds += ["join"] * halve_chips + ["last"]

    def pass_on(self, value, mask):
        return lax.ppermute(value, "row", partner_pairs(self.devices, mask))

    def round(self, count=1):
        for _ in range(count):
            if not self.rounds:
                return
            kind = self.rounds.pop(0)
            line, (core_bit, chip_bit) = self.line, self.bits
            if kind == "core":
                got = self.pass_on(self.theirs, 1)
                if self.rounds[0] == "halve":
                    self.mine, self.theirs = add_and_halve(line, chip_bit, self.mine, got)
                else:
                    self.mine, self.theirs = add_two(line, self.mine, got), None
            elif kind == "halve":
                self.mine = add_two(line, self.mine, self.pass_on(self.theirs, 2))
                self.theirs = None
            elif kind == "join":
                self.mine = join_halves(line, chip_bit, self.mine, self.pass_on(self.mine, 2))
            elif kind == "last":
                self.mine = join_halves(line, core_bit, self.mine, self.pass_on(self.mine, 1))
            else:
                self.mine = add_two(line, self.mine, self.pass_on(self.mine, kind))

    def held(self):
        return [self.mine] if self.theirs is None else [self.mine, self.theirs]

    def hold(self, values):
        self.mine = values[0]
        if self.theirs is not None:
            self.theirs = values[1]


def gate_all(parts, extra=(), events=()):
    lists = [p.held() for p in parts]
    flat = [v for values in lists for v in values] + list(extra)
    flat = gate(flat, events)
    at = 0
    for p, values in zip(parts, lists):
        p.hold(flat[at : at + len(values)])
        at += len(values)
    return flat[at:]


def encode(values):
    size = jnp.abs(values)
    most = jnp.max(size, axis=0, keepdims=True)
    level = size / jnp.maximum(most, 1e-37)
    power = jnp.exp((level * code_span - code_middle) * ln2)
    return jnp.where(values < 0.0, -power, power).astype(jnp.bfloat16), most


def decode(code, most):
    code = code.astype(jnp.float32)
    level = (jnp.log(jnp.abs(code)) * (1.0 / ln2) + code_middle) * (1.0 / code_span)
    return jnp.where(code < 0.0, -level, level) * most


def write_rows(rows):
    at = lax.broadcasted_iota(jnp.int32, (scale_rows, rows[0].shape[1]), 0)
    block = jnp.zeros(at.shape, jnp.float32)
    for i, row in enumerate(rows):
        high = row.astype(jnp.bfloat16).astype(jnp.float32)
        block = jnp.where(at == 2 * i, high, block)
        block = jnp.where(at == 2 * i + 1, row - high, block)
    return block.astype(jnp.bfloat16)


def read_row(block, i):
    block = block.astype(jnp.float32)
    return block[2 * i : 2 * i + 1] + block[2 * i + 1 : 2 * i + 2]


def pack(line, values, mine, got, extra):
    rows, rank = values.shape
    sum_rows = mine.shape[0]
    size = rows + scale_rows + sum_rows
    more = [] if extra is None else [extra]

    def kernel(line_ref, values_ref, mine_ref, got_ref, *refs):
        out_ref = refs[-1]
        code, most = encode(values_ref[...])
        sum_code, sum_most = encode(mine_ref[...] + got_ref[...])
        scales = [most, sum_most] + ([refs[0][:1, :]] if more else [])
        out_ref[:rows, :] = code
        out_ref[rows : rows + scale_rows, :] = write_rows(scales)
        out_ref[rows + scale_rows :, :] = sum_code

    return small_kernel(
        kernel,
        jax.ShapeDtypeStruct((size, rank), jnp.bfloat16),
        (line, values, mine, got, *more),
        "pack",
    )


def turn(line, snapshots, basis):
    windows, rows, count = snapshots.shape

    def kernel(line_ref, snap_ref, basis_ref, out_ref, snap_copy_ref, basis_copy_ref):
        for w in range(windows):
            out_ref[w] = snap_ref[w].T
        snap_copy_ref[...] = snap_ref[...]
        basis_copy_ref[...] = basis_ref[...]

    shapes = (
        jax.ShapeDtypeStruct((windows, count, rows), snapshots.dtype),
        jax.ShapeDtypeStruct(snapshots.shape, snapshots.dtype),
        f32(*basis.shape),
    )
    return small_kernel(kernel, shapes, (line, snapshots, basis), "turn")


def first_sums(line, bits, snapshots, basis, share):
    _, _, count = snapshots.shape
    rank = basis.shape[1]
    half = f32(count // 2, rank)

    def kernel(line_ref, snap_ref, basis_ref, share_ref, mine_ref, theirs_ref, part):
        part[...] = dot2(snap_ref[0], basis_ref[...], lead)
        store_halves(line_ref, bits[0], part, mine_ref, theirs_ref)

    return pl.pallas_call(
        kernel,
        out_shape=(half, half),
        in_specs=[in_smem, in_vmem, in_vmem, in_vmem],
        out_specs=(in_vmem, in_vmem),
        scratch_shapes=[pltpu.VMEM((count, rank), jnp.float32)],
        compiler_params=params,
        name="first_sums",
    )(line, snapshots, basis, share)


def local_trace(line, prior_cov, snapshots):
    windows, rows, count = snapshots.shape

    def total(x):
        return jnp.sum(jnp.sum(x, axis=0, keepdims=True), axis=1, keepdims=True)

    def kernel(line_ref, cov_ref, snap_ref, out_ref):
        row_at = lax.broadcasted_iota(jnp.int32, (128, 128), 0)
        col_at = lax.broadcasted_iota(jnp.int32, (128, 128), 1)
        diagonal = jnp.zeros((128, 128), jnp.float32)
        for at in range(0, rows, 128):
            first = pl.multiple_of(line_ref[0, 0] + at, 128)
            corner = cov_ref[at : at + 128, pl.ds(first, 128)]
            diagonal = diagonal + jnp.where(row_at == col_at, corner, 0.0)
        prior = total(diagonal)
        trace = prior
        for w in range(windows):
            snap = snap_ref[w].astype(jnp.float32)
            trace = forget_factor * trace + total(snap * snap) * (1.0 / count)
        at = lax.broadcasted_iota(jnp.int32, out_ref.shape, 0)
        out_ref[...] = jnp.where(at == 0, trace, prior * (1.0 / rows))

    return small_kernel(kernel, f32(8, 128), (line, prior_cov, snapshots), "local_trace")


def add_products(line_ref, base, cov_ref, block_refs, state, mean):
    running, own, other = state[:3]
    rows, rank = running.shape
    for at, block_ref in enumerate(block_refs):
        first = pl.multiple_of(line_ref[0, base + at], 128)
        scales = block_ref[rows : rows + scale_rows, :]
        block = decode(block_ref[:rows, :], read_row(scales, 0))
        piece = decode(block_ref[rows + scale_rows :, :], read_row(scales, 1))
        if at % 2 == 0:
            own = own + piece
        else:
            other = other + piece
        high, low = split(block)
        if mean is not None:
            gram, trace = state[3:]
            both = jnp.concatenate([high, low], axis=1)
            square = dot(high, both, lead)
            gram = gram + (square[:, :rank] + (square[:, rank:] + dot(low, high, lead)))
            trace = trace + read_row(scales, 2)
            state = (running, own, other, gram, trace)
            high, low = split(block * (1.0 / mean))
        both = jnp.concatenate([high, low], axis=1)
        cov_high, cov_low = split(cov_ref[:, pl.ds(first, rows)])
        wide = dot(cov_high, both, inner)
        running = running + (wide[:, :rank] + (wide[:, rank:] + dot(cov_low, high, inner)))
    return (running, own, other) + tuple(state[3:])


def state_shapes(rows, rank, sum_rows, last):
    shapes = [f32(n, rank) for n in (rows, sum_rows, sum_rows)]
    return shapes + ([f32(rank, rank), f32(1, rank)] if last else [])


def product_part(line, base, prior_cov, blocks, state, sum_rows, share, carried):
    count = len(blocks)
    last = share is not None
    shapes = state_shapes(prior_cov.shape[0], blocks[0].shape[1], sum_rows, last)
    outs = len(shapes)
    shapes += [jax.ShapeDtypeStruct(v.shape, v.dtype) for v in carried]
    more = ([share] if last else []) + list(state or [])

    def kernel(line_ref, cov_ref, *refs):
        block_refs, refs = refs[:count], refs[count:]
        carried_refs, refs = refs[: len(carried)], refs[len(carried) :]
        given, out_refs = refs[: -len(shapes)], refs[-len(shapes) :]
        for carried_ref, out_ref in zip(carried_refs, out_refs[outs:]):
            out_ref[...] = carried_ref[...]
        mean = None
        if last:
            mean, given = given[0][1:2, :1], given[1:]
        old = [r[...] for r in given] or [jnp.zeros(v.shape, jnp.float32) for v in shapes[:outs]]
        new = add_products(line_ref, base, cov_ref, block_refs, tuple(old), mean)
        for out_ref, value in zip(out_refs[:outs], new):
            out_ref[...] = value

    results = small_kernel(
        kernel, tuple(shapes), (line, prior_cov, *blocks, *carried, *more), "product_part"
    )
    return list(results[:outs]), list(results[outs:])


def product_end(line, bits, base, prior_cov, blocks, state, snapshots, window, share):
    rows, order = prior_cov.shape
    rank = blocks[0].shape[1]
    windows, _, snap_count = snapshots.shape
    count = len(blocks)
    last = share is not None
    sum_rows = state[1].shape[0]
    inv_snap = 1.0 / snap_count
    parts = len(state)
    more = [share] if last else []
    shapes = (f32(rows, rank),)
    if last:
        shapes += (f32(rank // 2, rank), f32(rank // 2, rank), f32(rank, rank))

    def kernel(line_ref, cov_ref, *refs):
        block_refs, refs = refs[:count], refs[count:]
        old = tuple(r[...] for r in refs[:parts])
        snap_ref, refs = refs[parts], refs[parts + 1 :]
        mean = None
        if last:
            mean, refs = refs[0][1:2, :1], refs[1:]
        outs, sums_buf, gram_buf = refs[: len(shapes)], refs[-2], refs[-1]
        new = add_products(line_ref, base, cov_ref, block_refs, old, mean)
        side = line_ref[0, bits[0]]
        sums_buf[pl.ds(pl.multiple_of(side * sum_rows, 8), sum_rows), :] = new[1]
        sums_buf[pl.ds(pl.multiple_of((1 - side) * sum_rows, 8), sum_rows), :] = new[2]
        applied = new[0] * forget_factor ** (window + 1)
        scale = 1.0
        if last:
            scale = float(order) / new[4]
            applied = applied * (scale * mean)
        for w in range(window + 1):
            at = w * snap_count
            total = sums_buf[at : at + snap_count, :] * scale
            weight = forget_factor ** (window - w) * inv_snap
            applied = applied + weight * dot2(snap_ref[w], total, inner)
        outs[0][...] = applied
        if last:
            gram_buf[...] = lax.dot_general(
                applied,
                applied,
                lead,
                precision=lax.Precision.HIGHEST,
                preferred_element_type=jnp.float32,
            )
            store_halves(line_ref, bits[0], gram_buf, outs[1], outs[2])
            outs[3][...] = new[3]

    return pl.pallas_call(
        kernel,
        out_shape=shapes,
        in_specs=[in_smem] + [in_vmem] * (2 + count + parts + len(more)),
        out_specs=tuple(in_vmem for _ in shapes),
        scratch_shapes=[
            pltpu.VMEM((2 * sum_rows, rank), jnp.float32),
            pltpu.VMEM((rank, rank), jnp.float32),
        ],
        compiler_params=params,
        name="product_end",
    )(line, prior_cov, *blocks, *state, snapshots, *more)


def window_sums(line, bits, applied, snapshots):
    windows, _, snap_count = snapshots.shape
    rank = applied.shape[1]
    total = windows * snap_count
    half = f32(total // 2, rank)

    def kernel(line_ref, applied_ref, snap_ref, mine_ref, theirs_ref, part):
        for w in range(windows):
            at = w * snap_count
            part[at : at + snap_count, :] = dot2(snap_ref[w], applied_ref[...], lead)
        store_halves(line_ref, bits[0], part, mine_ref, theirs_ref)

    return pl.pallas_call(
        kernel,
        out_shape=(half, half),
        in_specs=[in_smem] + [in_vmem] * 2,
        out_specs=(in_vmem, in_vmem),
        scratch_shapes=[pltpu.VMEM((total, rank), jnp.float32)],
        compiler_params=params,
        name="window_sums",
    )(line, applied, snapshots)


panel = 8


def inverse_factor(gram):
    rank = gram.shape[0]
    eye = lax.broadcasted_iota(jnp.int32, (rank, rank), 0) == lax.broadcasted_iota(
        jnp.int32, (rank, rank), 1
    )
    diagonal = jnp.where(eye, gram, 0.0)
    down = lax.rsqrt(jnp.sum(diagonal, axis=1, keepdims=True))
    along = lax.rsqrt(jnp.sum(diagonal, axis=0, keepdims=True))
    gram = gram * down * along
    start = jnp.where(eye, along, 0.0)
    count = rank // panel
    rows = [gram[i * panel : (i + 1) * panel] for i in range(count)]
    sides = [start[i * panel : (i + 1) * panel] for i in range(count)]
    sub = lax.broadcasted_iota(jnp.int32, (panel, rank), 0)
    finished = []
    for top in range(count):
        first = top * panel
        spread = {
            i: [
                jnp.broadcast_to(rows[i][:, first + k : first + k + 1], (panel, rank))
                for k in range(panel)
            ]
            for i in range(top, count)
        }
        done = jnp.zeros((panel, rank), jnp.float32)
        for j in range(0, panel, 2):
            row0, row1 = rows[top][j : j + 1], rows[top][j + 1 : j + 2]
            side0, side1 = sides[top][j : j + 1], sides[top][j + 1 : j + 2]
            lead_columns = spread[top]
            a = lead_columns[j][j : j + 1]
            b = lead_columns[j][j + 1 : j + 2]
            c = lead_columns[j + 1][j + 1 : j + 2]
            over = 1.0 / (a * c - b * b)
            a_over, b_over, c_over = a * over, b * over, c * over
            root = lax.rsqrt(a)
            ratio = b * root * root
            done = jnp.where(sub == j, side0 * root, done)
            done = jnp.where(
                sub == j + 1, (side1 - ratio * side0) * lax.rsqrt(c - ratio * b), done
            )
            heads = [
                (lead_columns[m][j : j + 1], lead_columns[m][j + 1 : j + 2]) for m in range(panel)
            ]
            for i in range(top, count):
                x0, x1 = spread[i][j], spread[i][j + 1]
                m0 = x0 * c_over - x1 * b_over
                m1 = x1 * a_over - x0 * b_over
                rows[i] = rows[i] - (m0 * row0 + m1 * row1)
                sides[i] = sides[i] - (m0 * side0 + m1 * side1)
                for m in range(j + 2, panel):
                    head0, head1 = heads[m]
                    spread[i][m] = spread[i][m] - (m0 * head0 + m1 * head1)
        finished.append(done)
    return jnp.concatenate(finished, axis=0)


def factor(line, gram):
    def kernel(line_ref, gram_ref, out_ref):
        out_ref[...] = inverse_factor(gram_ref[...])

    return small_kernel(kernel, f32(*gram.shape), (line, gram), "factor")


def finish(line, bits, gram, theirs, first, applied):
    rank = applied.shape[1]
    half = rank // 2

    def kernel(line_ref, gram_ref, theirs_ref, first_ref, applied_ref, out_ref, buf):
        side = line_ref[0, bits[0]]
        buf[pl.ds(pl.multiple_of(side * half, 8), half), :] = gram_ref[...]
        buf[pl.ds(pl.multiple_of((1 - side) * half, 8), half), :] = theirs_ref[...]
        first = first_ref[...]

        def exact(a, b, dims):
            return lax.dot_general(
                a,
                b,
                dims,
                precision=lax.Precision.HIGHEST,
                preferred_element_type=jnp.float32,
            )

        second_gram = exact(exact(first, buf[...], inner), first, trail)
        second = inverse_factor(second_gram)
        out_ref[...] = dot3(applied_ref[...], exact(second, first, inner), trail)

    return pl.pallas_call(
        kernel,
        out_shape=f32(*applied.shape),
        in_specs=[in_smem] + [in_vmem] * 4,
        out_specs=in_vmem,
        scratch_shapes=[pltpu.VMEM((rank, rank), jnp.float32)],
        compiler_params=params,
        name="finish",
    )(line, gram, theirs, first, applied)


def covariance_part(line, numbers, prior_cov, snapshots, blocks, filled):
    rows, _ = prior_cov.shape
    windows, _, snap_count = snapshots.shape
    count = len(blocks)
    more = [] if filled is None else [filled]
    inv_snap = 1.0 / snap_count

    def kernel(line_ref, cov_ref, snap_ref, *refs):
        block_refs, refs = refs[:count], refs[count + len(more) :]
        out_ref, out_bufs, sems = refs[0], refs[1:-1], refs[-1]
        copies = []
        for at in range(count):
            width = block_refs[at].shape[2]
            first = pl.multiple_of(line_ref[0, numbers[at]], 128)
            columns = pl.ds(first, width)
            total = cov_ref[:, columns] * forget_factor**windows
            for w in range(windows):
                weight = forget_factor ** (windows - 1 - w) * inv_snap
                total = total + weight * dot(snap_ref[w], block_refs[at][w], inner)
            out_bufs[at][...] = total
            copy = pltpu.make_async_copy(out_bufs[at], out_ref.at[:, columns], sems.at[at])
            copy.start()
            copies.append(copy)
        for copy in copies:
            copy.wait()

    return pl.pallas_call(
        kernel,
        out_shape=f32(*prior_cov.shape),
        in_specs=[in_smem] + [in_vmem] * (2 + count) + [in_hbm] * len(more),
        out_specs=in_hbm,
        scratch_shapes=[pltpu.VMEM((rows, b.shape[2]), jnp.float32) for b in blocks]
        + [pltpu.SemaphoreType.DMA((count,))],
        input_output_aliases={3 + count: 0} if more else {},
        compiler_params=params,
        name="covariance_part",
    )(line, prior_cov, snapshots, *blocks, *more)


def local(devices, prior_cov, snapshots, prior_basis):
    rows = prior_cov.shape[0]
    rank = prior_basis.shape[1]
    windows, _, snap_count = snapshots.shape
    table = ring_table(devices, rows)
    me = lax.axis_index("row")
    line = lax.dynamic_slice_in_dim(jnp.asarray(table), me, 1, axis=0)
    entries = table.shape[1]
    bits = (entries - 2, entries - 1)
    steps = devices // 4
    starts = [0] + [2 + 4 * at for at in range(steps)]
    swap = partner_pairs(devices, 1)

    def fill(filled, numbers):
        blocks = [b for group in snap_ring.groups for b in group]
        chosen = [blocks[n] for n in numbers]
        return covariance_part(line, numbers, prior_cov, snapshots, chosen, filled)

    turned, snapshots, values = turn(line, snapshots, prior_basis)
    snap_ring = Ring(line, bits, turned, devices)
    snap_ring.pass_on()
    snap_ring.step()
    next_share = local_trace(line, prior_cov, snapshots)
    mine, theirs = first_sums(line, bits, snapshots, values, next_share)
    share = new_cov = None
    for window in range(windows):
        got = lax.ppermute(theirs, "row", swap)
        if window == 1:
            (values, new_cov) = gate_all([snap_ring], [values, new_cov])
        ring = Ring(line, bits, pack(line, values, mine, got, share), devices)
        sum_rows = mine.shape[0]
        state = None
        for phase in range(1, steps + 1):
            sent = ring.recent
            ring.step()
            arrived, ring.recent = ring.recent, sent
            extra, waiting = [], [ring]
            if phase == 1:
                ring.pass_on()
                if window == 0:
                    waiting.append(snap_ring)
                else:
                    snap_ring.recent = gate(snap_ring.recent, [sent[0]])
                    snap_ring.pass_on()
                    waiting.append(snap_ring)
                    new_cov = fill(new_cov, [6, 8])
                    extra.append(new_cov)
            else:
                state, _ = product_part(
                    line,
                    starts[phase - 2],
                    prior_cov,
                    ring.groups[phase - 2],
                    state,
                    sum_rows,
                    share,
                    [],
                )
                ring.pass_on()
                arrived = gate(arrived, [state[0]])
                extra += state
                if window == 0 and phase == steps - 1:
                    snap_ring.new_recent = True
                    waiting.append(snap_ring)
                if phase == steps:
                    if window == 0:
                        snap_ring.pass_on()
                    snap_ring.new_recent = True
                    waiting.append(snap_ring)
            ring.recent = arrived
            extra = gate_all(waiting, extra)
            if window == 1 and phase == 1:
                new_cov = extra.pop()
            state = extra or None
        snap_ring.step()
        state, _ = product_part(
            line,
            starts[steps - 1],
            prior_cov,
            ring.groups[steps - 1],
            state,
            sum_rows,
            share,
            [],
        )
        ring.pass_on()
        result = product_end(
            line,
            bits,
            starts[steps],
            prior_cov,
            ring.groups[steps],
            state,
            snapshots,
            window,
            share,
        )
        if window == 0:
            (values,) = result
            share = next_share
            mine, theirs = window_sums(line, bits, values, snapshots)
            new_cov = fill(None, range(6))
    applied, mine, theirs, first_gram = result
    total = Total(line, bits, mine, theirs, devices, False)
    total.rounds.pop()
    total.round()
    first = factor(line, first_gram)
    while snap_ring.done < steps - 1:
        (first,) = gate_all([total, snap_ring], [first])
        snap_ring.pass_on()
        snap_ring.step()
    (first, new_cov) = gate_all([total, snap_ring], [first, new_cov])

    end = 4 * steps
    snap_ring.step()
    arrived, snap_ring.recent = snap_ring.recent, snap_ring.full
    snap_ring.pass_on()
    snap_ring.recent = arrived
    total.round()
    new_cov = fill(new_cov, [7, 9] + list(range(10, end - 6)))
    new_cov = fill(new_cov, [end - 6, end - 4])
    (first, new_cov) = gate_all([total, snap_ring], [first, new_cov])
    snap_ring.pass_on()
    total.round()
    new_cov = fill(new_cov, [end - 5, end - 3])
    (first, new_cov) = gate_all([total, snap_ring], [first, new_cov])
    while total.rounds:
        total.round()
    new_cov = fill(new_cov, [end - 2, end - 1])
    (first, new_cov) = gate_all([total], [first, new_cov])
    theirs = lax.ppermute(total.mine, "row", swap)
    new_basis = finish(line, bits, total.mine, theirs, first, applied)
    return (new_cov, new_basis)


def solution(mesh):
    return jax.shard_map(
        functools.partial(local, mesh.shape["row"]),
        mesh=mesh,
        in_specs=(
            P(("band", "row"), None),
            P(None, ("band", "row"), None),
            P(("band", "row"), None),
        ),
        out_specs=(P(("band", "row"), None), P(("band", "row"), None)),
        check_vma=False,
    )
```

```python
import functools

import jax
import jax.numpy as jnp
import numpy as np
from jax import lax
from jax.experimental import pallas as pl
from jax.experimental.pallas import tpu as pltpu
from jax.sharding import PartitionSpec as P

forget_factor = 0.9
code_span = 240.0
code_middle = 120.0
scale_rows = 16
ln2 = 0.6931471805599453
in_vmem = pl.BlockSpec(memory_space=pltpu.VMEM)
anywhere = pl.BlockSpec(memory_space=pl.ANY)
in_hbm = pl.BlockSpec(memory_space=pltpu.HBM)
in_smem = pl.BlockSpec(memory_space=pltpu.SMEM)
params = pltpu.CompilerParams(vmem_limit_bytes=16 * 2**20)

inner = (((1,), (0,)), ((), ()))
lead = (((0,), (0,)), ((), ()))
trail = (((1,), (1,)), ((), ()))


def dot(a, b, dims):
    return lax.dot_general(a, b, dims, preferred_element_type=jnp.float32)


def split(x):
    high = x.astype(jnp.bfloat16)
    return high, (x - high.astype(jnp.float32)).astype(jnp.bfloat16)


def dot3(a, b, dims):
    a_high, a_low = split(a)
    b_high, b_low = split(b)
    return dot(a_high, b_high, dims) + (dot(a_high, b_low, dims) + dot(a_low, b_high, dims))


def dot2(a, b, dims):
    b_high, b_low = split(b)
    return dot(a, b_high, dims) + dot(a, b_low, dims)


def gate(values, events=()):
    count = len(values)

    def kernel(*refs):
        pass

    return list(
        pl.pallas_call(
            kernel,
            out_shape=tuple(jax.ShapeDtypeStruct(v.shape, v.dtype) for v in values),
            in_specs=[anywhere] * (count + len(events)),
            out_specs=(anywhere,) * count,
            input_output_aliases={i: i for i in range(count)},
            compiler_params=params,
            name="gate",
        )(*values, *events)
    )


def ring_order(devices):
    chips = devices // 2
    return list(range(0, chips, 2)) + list(range(chips - 1, 0, -2))


def ring_pairs(devices, way):
    order = ring_order(devices)
    chips = len(order)
    pairs = []
    for at in range(chips):
        for core in range(2):
            pairs.append((2 * order[at] + core, 2 * order[(at + way) % chips] + core))
    return pairs


def partner_pairs(devices, mask):
    return [(i, i ^ mask) for i in range(devices)]


def ring_table(devices, rows):
    order = ring_order(devices)
    chips = len(order)
    table = []
    for me in range(devices):
        at, core = order.index(me // 2), me % 2
        line = [me * rows, (me ^ 1) * rows]
        for step in range(1, chips // 2):
            for there in (at - step, at + step):
                chip = order[there % chips]
                line += [(2 * chip + core) * rows, (2 * chip + 1 - core) * rows]
        chip = order[(at + chips // 2) % chips]
        line += [(2 * chip + core) * rows, (2 * chip + 1 - core) * rows]
        line += [core, (me // 2) % 2]
        table.append(line)
    return np.array(table, np.int32)


class Ring:
    def __init__(self, line, bits, block, devices):
        self.line, self.bits = line, bits
        self.forth, self.back = ring_pairs(devices, 1), ring_pairs(devices, -1)
        self.apart = [p for p in self.forth if p[0] % 2 == 0] + [
            p for p in self.back if p[0] % 2 == 1
        ]
        self.swap = partner_pairs(devices, 1)
        self.steps = devices // 4
        self.done = 0
        self.chosen = None
        self.recent = [block]
        self.groups = []
        self.new_recent = self.new_swapped = False

    def pass_on(self, copies=None):
        group = []
        for block, copy in zip(self.recent, copies or self.recent):
            group += [block, lax.ppermute(copy, "row", self.swap)]
        self.groups.append(group)
        self.new_swapped = True

    def pass_on_full(self, copies=None):
        arrived, self.recent = self.recent, self.full
        self.pass_on(copies)
        self.recent = arrived

    def step(self):
        self.done += 1
        self.new_recent = True
        ahead, behind = self.recent[0], self.recent[-1]
        self.full = self.recent
        if self.done == self.steps:
            block = ahead if self.chosen is None else self.chosen
            if self.chosen is None and len(self.recent) == 2:
                block = choose(self.line, self.bits[0], ahead, behind)
            self.recent = [lax.ppermute(block, "row", self.apart)]
        else:
            self.recent = [
                lax.ppermute(ahead, "row", self.forth),
                lax.ppermute(behind, "row", self.back),
            ]

    def held(self):
        return (self.recent if self.new_recent else []) + (
            self.groups[-1][1::2] if self.new_swapped else []
        )

    def hold(self, values):
        values = list(values)
        if self.new_recent:
            old, count = self.recent, len(self.recent)
            self.recent, values = values[:count], values[count:]
            for group in self.groups:
                for at, block in enumerate(group):
                    for before, now in zip(old, self.recent):
                        if block is before:
                            group[at] = now
        if self.new_swapped:
            self.groups[-1][1::2] = values
        self.new_recent = self.new_swapped = False


def small_kernel(kernel, out_shape, args, name):
    multiple = isinstance(out_shape, tuple)
    return pl.pallas_call(
        kernel,
        out_shape=out_shape,
        in_specs=[in_smem] + [in_vmem] * (len(args) - 1),
        out_specs=tuple(in_vmem for _ in out_shape) if multiple else in_vmem,
        compiler_params=params,
        name=name,
    )(*args)


def f32(*shape):
    return jax.ShapeDtypeStruct(shape, jnp.float32)


def choose(line, bit, first, second):
    def kernel(line_ref, first_ref, second_ref, out_ref):
        @pl.when(line_ref[0, bit] == 0)
        def _():
            out_ref[...] = first_ref[...]

        @pl.when(line_ref[0, bit] == 1)
        def _():
            out_ref[...] = second_ref[...]

    shape = jax.ShapeDtypeStruct(first.shape, first.dtype)
    return small_kernel(kernel, shape, (line, first, second), "choose")


def store_halves(line_ref, bit, value_ref, mine_ref, theirs_ref):
    half = mine_ref.shape[0]
    side = line_ref[0, bit]
    mine_ref[...] = value_ref[pl.ds(pl.multiple_of(side * half, 8), half), :]
    theirs_ref[...] = value_ref[pl.ds(pl.multiple_of((1 - side) * half, 8), half), :]


def add_all(line, values):
    def kernel(line_ref, *refs):
        total = refs[0][...]
        for ref in refs[1:-1]:
            total = total + ref[...]
        refs[-1][...] = total

    return small_kernel(kernel, f32(*values[0].shape), (line, *values), "add_all")


def add_and_halve(line, bit, a, b):
    half = f32(a.shape[0] // 2, a.shape[1])

    def kernel(line_ref, a_ref, b_ref, mine_ref, theirs_ref):
        size = mine_ref.shape[0]
        side = line_ref[0, bit]
        for out_ref, which in ((mine_ref, side), (theirs_ref, 1 - side)):
            rows = pl.ds(pl.multiple_of(which * size, 8), size)
            out_ref[...] = a_ref[rows, :] + b_ref[rows, :]

    return small_kernel(kernel, (half, half), (line, a, b), "add_and_halve")


def join_halves(line, bit, mine, theirs):
    def kernel(line_ref, mine_ref, theirs_ref, out_ref):
        size = mine_ref.shape[0]
        side = line_ref[0, bit]
        out_ref[pl.ds(pl.multiple_of(side * size, 8), size), :] = mine_ref[...]
        out_ref[pl.ds(pl.multiple_of((1 - side) * size, 8), size), :] = theirs_ref[...]

    shape = f32(2 * mine.shape[0], mine.shape[1])
    return small_kernel(kernel, shape, (line, mine, theirs), "join_halves")


class Total:
    def __init__(self, line, bits, mine, theirs, devices, halve_chips):
        self.line, self.bits, self.devices = line, bits, devices
        self.mine, self.theirs = mine, theirs
        first = 4 if halve_chips else 2
        self.rounds = ["core"] + ["halve"] * halve_chips
        while first < devices:
            self.rounds.append(first)
            first *= 2
        self.rounds += ["join"] * halve_chips + ["last"]

    def pass_on(self, value, mask):
        return lax.ppermute(value, "row", partner_pairs(self.devices, mask))

    def round(self, count=1):
        for _ in range(count):
            if not self.rounds:
                return
            kind = self.rounds.pop(0)
            line, (core_bit, chip_bit) = self.line, self.bits
            if kind == "core":
                got = self.pass_on(self.theirs, 1)
                if self.rounds[0] == "halve":
                    self.mine, self.theirs = add_and_halve(line, chip_bit, self.mine, got)
                else:
                    self.mine, self.theirs = add_all(line, [self.mine, got]), None
            elif kind == "halve":
                self.mine = add_all(line, [self.mine, self.pass_on(self.theirs, 2)])
                self.theirs = None
            elif kind == "join":
                self.mine = join_halves(line, chip_bit, self.mine, self.pass_on(self.mine, 2))
            elif kind == "last":
                self.mine = join_halves(line, core_bit, self.mine, self.pass_on(self.mine, 1))
            else:
                self.mine = add_all(line, [self.mine, self.pass_on(self.mine, kind)])

    def held(self):
        return [self.mine] if self.theirs is None else [self.mine, self.theirs]

    def hold(self, values):
        self.mine = values[0]
        if self.theirs is not None:
            self.theirs = values[1]


def gate_all(parts, extra=(), events=()):
    lists = [p.held() for p in parts]
    flat = [v for values in lists for v in values] + list(extra)
    flat = gate(flat, events)
    at = 0
    for p, values in zip(parts, lists):
        p.hold(flat[at : at + len(values)])
        at += len(values)
    return flat[at:]


def encode(values):
    size = jnp.abs(values)
    most = jnp.max(size, axis=0, keepdims=True)
    level = size / jnp.maximum(most, 1e-37)
    power = jnp.exp((level * code_span - code_middle) * ln2)
    return jnp.where(values < 0.0, -power, power).astype(jnp.bfloat16), most


def decode(code, most):
    code = code.astype(jnp.float32)
    level = (jnp.log(jnp.abs(code)) * (1.0 / ln2) + code_middle) * (1.0 / code_span)
    return jnp.where(code < 0.0, -level, level) * most


def write_rows(rows):
    at = lax.broadcasted_iota(jnp.int32, (scale_rows, rows[0].shape[1]), 0)
    block = jnp.zeros(at.shape, jnp.float32)
    for i, row in enumerate(rows):
        high = row.astype(jnp.bfloat16).astype(jnp.float32)
        block = jnp.where(at == 2 * i, high, block)
        block = jnp.where(at == 2 * i + 1, row - high, block)
    return block.astype(jnp.bfloat16)


def read_row(block, i):
    block = block.astype(jnp.float32)
    return block[2 * i : 2 * i + 1] + block[2 * i + 1 : 2 * i + 2]


def pack(line, values, mine, got, extra):
    rows, rank = values.shape
    sum_rows = mine.shape[0]
    size = rows + scale_rows + sum_rows
    more = [] if extra is None else [extra]

    def kernel(line_ref, values_ref, mine_ref, got_ref, *refs):
        out_ref = refs[-1]
        code, most = encode(values_ref[...])
        sum_code, sum_most = encode(mine_ref[...] + got_ref[...])
        scales = [most, sum_most] + ([refs[0][:1, :]] if more else [])
        out_ref[:rows, :] = code
        out_ref[rows : rows + scale_rows, :] = write_rows(scales)
        out_ref[rows + scale_rows :, :] = sum_code

    return small_kernel(
        kernel,
        jax.ShapeDtypeStruct((size, rank), jnp.bfloat16),
        (line, values, mine, got, *more),
        "pack",
    )


def first_sums(line, bits, snapshots, basis):
    _, _, count = snapshots.shape
    rank = basis.shape[1]
    half = f32(count // 2, rank)

    def kernel(
        line_ref, snap_ref, basis_ref, mine_ref, theirs_ref, snap_copy_ref, basis_copy_ref, part
    ):
        part[...] = dot2(snap_ref[0], basis_ref[...], lead)
        store_halves(line_ref, bits[0], part, mine_ref, theirs_ref)
        snap_copy_ref[...] = snap_ref[...]
        basis_copy_ref[...] = basis_ref[...]

    return pl.pallas_call(
        kernel,
        out_shape=(
            half,
            half,
            jax.ShapeDtypeStruct(snapshots.shape, snapshots.dtype),
            f32(*basis.shape),
        ),
        in_specs=[in_smem, in_vmem, in_vmem],
        out_specs=(in_vmem,) * 4,
        scratch_shapes=[pltpu.VMEM((count, rank), jnp.float32)],
        compiler_params=params,
        name="first_sums",
    )(line, snapshots, basis)


def local_trace(line, prior_cov, snapshots, event):
    windows, rows, count = snapshots.shape

    def total(x):
        return jnp.sum(jnp.sum(x, axis=0, keepdims=True), axis=1, keepdims=True)

    def kernel(line_ref, cov_ref, snap_ref, event_ref, out_ref, copy_ref):
        copy_ref[...] = snap_ref[...]
        row_at = lax.broadcasted_iota(jnp.int32, (128, 128), 0)
        col_at = lax.broadcasted_iota(jnp.int32, (128, 128), 1)
        diagonal = jnp.zeros((128, 128), jnp.float32)
        for at in range(0, rows, 128):
            first = pl.multiple_of(line_ref[0, 0] + at, 128)
            corner = cov_ref[at : at + 128, pl.ds(first, 128)]
            diagonal = diagonal + jnp.where(row_at == col_at, corner, 0.0)
        prior = total(diagonal)
        trace = prior
        for w in range(windows):
            snap = snap_ref[w].astype(jnp.float32)
            trace = forget_factor * trace + total(snap * snap) * (1.0 / count)
        at = lax.broadcasted_iota(jnp.int32, out_ref.shape, 0)
        out_ref[...] = jnp.where(at == 0, trace, prior * (1.0 / rows))

    shapes = (f32(8, 128), jax.ShapeDtypeStruct(snapshots.shape, snapshots.dtype))
    return small_kernel(kernel, shapes, (line, prior_cov, snapshots, event), "local_trace")


def add_products(line_ref, base, cov_ref, block_refs, state, mean):
    running, own, other = state[:3]
    rows, rank = running.shape
    for at, block_ref in enumerate(block_refs):
        first = pl.multiple_of(line_ref[0, base + at], 128)
        scales = block_ref[rows : rows + scale_rows, :]
        block = decode(block_ref[:rows, :], read_row(scales, 0))
        piece = decode(block_ref[rows + scale_rows :, :], read_row(scales, 1))
        if at % 2 == 0:
            own = own + piece
        else:
            other = other + piece
        high, low = split(block)
        if mean is not None:
            gram, trace = state[3:]
            both = jnp.concatenate([high, low], axis=1)
            square = dot(high, both, lead)
            gram = gram + (square[:, :rank] + (square[:, rank:] + dot(low, high, lead)))
            trace = trace + read_row(scales, 2)
            state = (running, own, other, gram, trace)
            high, low = split(block * (1.0 / mean))
        both = jnp.concatenate([high, low], axis=1)
        cov_high, cov_low = split(cov_ref[:, pl.ds(first, rows)])
        wide = dot(cov_high, both, inner)
        running = running + (wide[:, :rank] + (wide[:, rank:] + dot(cov_low, high, inner)))
    return (running, own, other) + tuple(state[3:])


def state_shapes(rows, rank, sum_rows, last):
    shapes = [f32(n, rank) for n in (rows, sum_rows, sum_rows)]
    return shapes + ([f32(rank, rank), f32(1, rank)] if last else [])


def product_part(line, base, prior_cov, blocks, state, sum_rows, share, carried):
    count = len(blocks)
    last = share is not None
    shapes = state_shapes(prior_cov.shape[0], blocks[0].shape[1], sum_rows, last)
    outs = len(shapes)
    shapes += [jax.ShapeDtypeStruct(v.shape, v.dtype) for v in carried]
    more = ([share] if last else []) + list(state or [])

    def kernel(line_ref, cov_ref, *refs):
        block_refs, refs = refs[:count], refs[count:]
        carried_refs, refs = refs[: len(carried)], refs[len(carried) :]
        given, out_refs = refs[: -len(shapes)], refs[-len(shapes) :]
        for carried_ref, out_ref in zip(carried_refs, out_refs[outs:]):
            out_ref[...] = carried_ref[...]
        mean = None
        if last:
            mean, given = given[0][1:2, :1], given[1:]
        old = [r[...] for r in given] or [jnp.zeros(v.shape, jnp.float32) for v in shapes[:outs]]
        new = add_products(line_ref, base, cov_ref, block_refs, tuple(old), mean)
        for out_ref, value in zip(out_refs[:outs], new):
            out_ref[...] = value

    results = small_kernel(
        kernel, tuple(shapes), (line, prior_cov, *blocks, *carried, *more), "product_part"
    )
    return list(results[:outs]), list(results[outs:])


def product_end(line, bits, base, prior_cov, blocks, state, snapshots, window, share):
    rows, order = prior_cov.shape
    rank = blocks[0].shape[1]
    windows, _, snap_count = snapshots.shape
    count = len(blocks)
    last = share is not None
    sum_rows = state[1].shape[0]
    inv_snap = 1.0 / snap_count
    parts = len(state)
    more = [share] if last else []
    shapes = (f32(rows, rank),)
    if last:
        shapes += (f32(rank // 2, rank), f32(rank // 2, rank), f32(rank, rank))

    def kernel(line_ref, cov_ref, *refs):
        block_refs, refs = refs[:count], refs[count:]
        old = tuple(r[...] for r in refs[:parts])
        snap_ref, refs = refs[parts], refs[parts + 1 :]
        mean = None
        if last:
            mean, refs = refs[0][1:2, :1], refs[1:]
        outs, sums_buf, gram_buf = refs[: len(shapes)], refs[-2], refs[-1]
        new = add_products(line_ref, base, cov_ref, block_refs, old, mean)
        side = line_ref[0, bits[0]]
        sums_buf[pl.ds(pl.multiple_of(side * sum_rows, 8), sum_rows), :] = new[1]
        sums_buf[pl.ds(pl.multiple_of((1 - side) * sum_rows, 8), sum_rows), :] = new[2]
        applied = new[0] * forget_factor ** (window + 1)
        scale = 1.0
        if last:
            scale = float(order) / new[4]
            applied = applied * (scale * mean)
        for w in range(window + 1):
            at = w * snap_count
            total = sums_buf[at : at + snap_count, :] * scale
            weight = forget_factor ** (window - w) * inv_snap
            applied = applied + weight * dot2(snap_ref[w], total, inner)
        outs[0][...] = applied
        if last:
            gram_buf[...] = lax.dot_general(
                applied,
                applied,
                lead,
                precision=lax.Precision.HIGHEST,
                preferred_element_type=jnp.float32,
            )
            store_halves(line_ref, bits[0], gram_buf, outs[1], outs[2])
            outs[3][...] = new[3]

    return pl.pallas_call(
        kernel,
        out_shape=shapes,
        in_specs=[in_smem] + [in_vmem] * (2 + count + parts + len(more)),
        out_specs=tuple(in_vmem for _ in shapes),
        scratch_shapes=[
            pltpu.VMEM((2 * sum_rows, rank), jnp.float32),
            pltpu.VMEM((rank, rank), jnp.float32),
        ],
        compiler_params=params,
        name="product_end",
    )(line, prior_cov, *blocks, *state, snapshots, *more)


def window_sums(line, bits, applied, snapshots):
    windows, _, snap_count = snapshots.shape
    rank = applied.shape[1]
    total = windows * snap_count
    half = f32(total // 2, rank)

    def kernel(line_ref, applied_ref, snap_ref, mine_ref, theirs_ref, part):
        for w in range(windows):
            at = w * snap_count
            part[at : at + snap_count, :] = dot2(snap_ref[w], applied_ref[...], lead)
        store_halves(line_ref, bits[0], part, mine_ref, theirs_ref)

    return pl.pallas_call(
        kernel,
        out_shape=(half, half),
        in_specs=[in_smem] + [in_vmem] * 2,
        out_specs=(in_vmem, in_vmem),
        scratch_shapes=[pltpu.VMEM((total, rank), jnp.float32)],
        compiler_params=params,
        name="window_sums",
    )(line, applied, snapshots)


panel = 8


def reciprocal(x):
    guess = pl.reciprocal(x, approx=True)
    guess = guess * (2.0 - x * guess)
    return guess * (2.0 - x * guess)


def inverse_factor(gram):
    rank = gram.shape[0]
    eye = lax.broadcasted_iota(jnp.int32, (rank, rank), 0) == lax.broadcasted_iota(
        jnp.int32, (rank, rank), 1
    )
    diagonal = jnp.where(eye, gram, 0.0)
    down = lax.rsqrt(jnp.sum(diagonal, axis=1, keepdims=True))
    along = lax.rsqrt(jnp.sum(diagonal, axis=0, keepdims=True))
    gram = gram * down * along
    start = jnp.where(eye, along, 0.0)
    count = rank // panel
    rows = [gram[i * panel : (i + 1) * panel] for i in range(count)]
    sides = [start[i * panel : (i + 1) * panel] for i in range(count)]
    sub = lax.broadcasted_iota(jnp.int32, (panel, rank), 0)
    finished = []
    for top in range(count):
        first = top * panel
        spread = {
            i: [
                jnp.broadcast_to(rows[i][:, first + k : first + k + 1], (panel, rank))
                for k in range(panel)
            ]
            for i in range(top, count)
        }
        done = jnp.zeros((panel, rank), jnp.float32)
        for j in range(0, panel, 2):
            row0, row1 = rows[top][j : j + 1], rows[top][j + 1 : j + 2]
            side0, side1 = sides[top][j : j + 1], sides[top][j + 1 : j + 2]
            lead_columns = spread[top]
            a = lead_columns[j][j : j + 1]
            b = lead_columns[j][j + 1 : j + 2]
            c = lead_columns[j + 1][j + 1 : j + 2]
            over = reciprocal(a * c - b * b)
            a_over, b_over, c_over = a * over, b * over, c * over
            root = lax.rsqrt(a)
            ratio = b * root * root
            done = jnp.where(sub == j, side0 * root, done)
            done = jnp.where(
                sub == j + 1, (side1 - ratio * side0) * lax.rsqrt(c - ratio * b), done
            )
            heads = [
                (lead_columns[m][j : j + 1], lead_columns[m][j + 1 : j + 2]) for m in range(panel)
            ]
            for i in range(top, count):
                x0, x1 = spread[i][j], spread[i][j + 1]
                m0 = x0 * c_over - x1 * b_over
                m1 = x1 * a_over - x0 * b_over
                rows[i] = rows[i] - (m0 * row0 + m1 * row1)
                sides[i] = sides[i] - (m0 * side0 + m1 * side1)
                for m in range(j + 2, panel):
                    head0, head1 = heads[m]
                    spread[i][m] = spread[i][m] - (m0 * head0 + m1 * head1)
        finished.append(done)
    return jnp.concatenate(finished, axis=0)


def factor(line, gram):
    def kernel(line_ref, gram_ref, out_ref):
        out_ref[...] = inverse_factor(gram_ref[...])

    return small_kernel(kernel, f32(*gram.shape), (line, gram), "factor")


def both_factors(line, bits, gram, theirs, first):
    rank = gram.shape[1]
    half = rank // 2

    def exact(a, b, dims):
        return lax.dot_general(
            a, b, dims, precision=lax.Precision.HIGHEST, preferred_element_type=jnp.float32
        )

    def kernel(line_ref, gram_ref, theirs_ref, first_ref, out_ref, buf):
        side = line_ref[0, bits[0]]
        buf[pl.ds(pl.multiple_of(side * half, 8), half), :] = gram_ref[...]
        buf[pl.ds(pl.multiple_of((1 - side) * half, 8), half), :] = theirs_ref[...]
        first = first_ref[...]
        second_gram = exact(exact(first, buf[...], inner), first, trail)
        out_ref[...] = exact(inverse_factor(second_gram), first, inner)

    return pl.pallas_call(
        kernel,
        out_shape=f32(rank, rank),
        in_specs=[in_smem] + [in_vmem] * 3,
        out_specs=in_vmem,
        scratch_shapes=[pltpu.VMEM((rank, rank), jnp.float32)],
        compiler_params=params,
        name="both_factors",
    )(line, gram, theirs, first)


def finish(line, factors, applied):
    def kernel(line_ref, factors_ref, applied_ref, out_ref):
        out_ref[...] = dot3(applied_ref[...], factors_ref[...], trail)

    return small_kernel(kernel, f32(*applied.shape), (line, factors, applied), "finish")


def covariance_part(line, numbers, prior_cov, snapshots, blocks, filled, carry=False):
    rows, _ = prior_cov.shape
    windows, _, snap_count = snapshots.shape
    count = len(blocks)
    more = [] if filled is None else [filled]
    copied = count if carry else 0
    inv_snap = 1.0 / snap_count

    def kernel(line_ref, cov_ref, snap_ref, *refs):
        block_refs, refs = refs[:count], refs[count + len(more) :]
        out_ref, copy_refs, refs = refs[0], refs[1 : 1 + copied], refs[1 + copied :]
        out_bufs, sems = refs[:-1], refs[-1]
        for block_ref, copy_ref in zip(block_refs, copy_refs):
            copy_ref[...] = block_ref[...]
        copies = []
        for at in range(count):
            width = block_refs[at].shape[1]
            first = pl.multiple_of(line_ref[0, numbers[at]], 128)
            columns = pl.ds(first, width)
            total = cov_ref[:, columns] * forget_factor**windows
            for w in range(windows):
                weight = forget_factor ** (windows - 1 - w) * inv_snap
                total = total + weight * dot(snap_ref[w], block_refs[at][w], trail)
            out_bufs[at][...] = total
            copy = pltpu.make_async_copy(out_bufs[at], out_ref.at[:, columns], sems.at[at])
            copy.start()
            copies.append(copy)
        for copy in copies:
            copy.wait()

    result = pl.pallas_call(
        kernel,
        out_shape=(f32(*prior_cov.shape),)
        + tuple(jax.ShapeDtypeStruct(b.shape, b.dtype) for b in blocks[:copied]),
        in_specs=[in_smem] + [in_vmem] * (2 + count) + [in_hbm] * len(more),
        out_specs=(in_hbm,) + (in_vmem,) * copied,
        scratch_shapes=[pltpu.VMEM((rows, b.shape[1]), jnp.float32) for b in blocks]
        + [pltpu.SemaphoreType.DMA((count,))],
        input_output_aliases={3 + count: 0} if more else {},
        compiler_params=params,
        name="covariance_part",
    )(line, prior_cov, snapshots, *blocks, *more)
    return (result[0], list(result[1:])) if carry else result[0]


def local(devices, prior_cov, snapshots, prior_basis):
    rows = prior_cov.shape[0]
    rank = prior_basis.shape[1]
    windows, _, snap_count = snapshots.shape
    table = ring_table(devices, rows)
    me = lax.axis_index("row")
    line = lax.dynamic_slice_in_dim(jnp.asarray(table), me, 1, axis=0)
    entries = table.shape[1]
    bits = (entries - 2, entries - 1)
    steps = devices // 4
    starts = [0] + [2 + 4 * at for at in range(steps)]
    swap = partner_pairs(devices, 1)

    def fill(filled, numbers):
        blocks = [b for group in snap_ring.groups for b in group]
        chosen = [blocks[n] for n in numbers]
        return covariance_part(line, numbers, prior_cov, snapshots, chosen, filled)

    def fill_own(filled, blocks, numbers):
        return covariance_part(line, numbers, prior_cov, snapshots, blocks, filled, True)

    end = 4 * steps
    snap_ring = Ring(line, bits, snapshots, devices)
    snap_ring.step()
    mine, theirs, snapshots, values = first_sums(line, bits, snapshots, prior_basis)
    share = new_cov = None
    for window in range(windows):
        got = lax.ppermute(theirs, "row", swap)
        if window == 1:
            (values,) = gate_all([snap_ring], [values])
        ring = Ring(line, bits, pack(line, values, mine, got, share), devices)
        sum_rows = mine.shape[0]
        state = None
        for phase in range(1, steps + 1):
            if phase == steps:
                chosen = choose(line, bits[0], *ring.recent)
                ring.chosen, *state = gate([chosen] + list(state))
                ready = state[0]
            sent = ring.recent
            ring.step()
            arrived, ring.recent = ring.recent, sent
            ring.pass_on()
            extra, waiting, filled = [], [ring], []
            if phase == 1:
                waiting.append(snap_ring)
                if window == 0:
                    next_share, snap_copy = local_trace(line, prior_cov, snapshots, sent[0])
                    arrived = gate(arrived, [next_share])
                    extra = [snap_copy]
                else:
                    snap_ring.recent = gate(snap_ring.recent, [sent[0]])
                    snap_ring.pass_on()
                    arrived = gate(arrived)
                    filled = [6, 8]
            else:
                state, _ = product_part(
                    line,
                    starts[phase - 2],
                    prior_cov,
                    ring.groups[phase - 2],
                    state,
                    sum_rows,
                    share,
                    [],
                )
                arrived = gate(arrived, [state[0]])
                extra += state
                if window == 0 and phase == 2:
                    snap_ring.full = [snap_copy]
                    snap_ring.pass_on_full()
                    snap_ring.groups[0][0] = snapshots
                    waiting.append(snap_ring)
                if window == 0 and phase == 3:
                    filled = [0, 1]
                if window == 1 and phase == 2:
                    filled = [7, 9]
                if window == 1 and phase == 3:
                    filled = [3, 5]
            if filled:
                new_cov = fill(new_cov, filled)
                extra.append(new_cov)
            ring.recent = arrived
            if phase == steps and window == 1:
                snap_ring.new_recent = True
                waiting.append(snap_ring)
            if phase == steps and window == 0:
                snap_ring.recent = gate(snap_ring.recent, [ready])
                snap_ring.step()
                if window == 0:
                    new_cov, copies = fill_own(new_cov, snap_ring.full, [2, 4])
                    extra += copies + [new_cov]
                    filled = [2, 4]
            extra = gate_all(waiting, extra)
            if window == 0 and phase == 1:
                snap_copy = extra.pop()
            if filled:
                new_cov = extra.pop()
            if window == 0 and phase == steps:
                extra, copies = extra[:-2], extra[-2:]
            state = extra or None
        if window == 0:
            snap_ring.pass_on_full(copies)
        else:
            snap_ring.step()
        state, _ = product_part(
            line,
            starts[steps - 1],
            prior_cov,
            ring.groups[steps - 1],
            state,
            sum_rows,
            share,
            [],
        )
        ring.pass_on()
        result = product_end(
            line,
            bits,
            starts[steps],
            prior_cov,
            ring.groups[steps],
            state,
            snapshots,
            window,
            share,
        )
        if window == 0:
            (values,) = result
            share = next_share
            mine, theirs = window_sums(line, bits, values, snapshots)
    applied, mine, theirs, first_gram = result
    total = Total(line, bits, mine, theirs, devices, False)
    total.rounds.pop()
    total.round()
    first = factor(line, first_gram)
    while snap_ring.done < steps - 1:
        (first,) = gate_all([total, snap_ring], [first])
        snap_ring.pass_on()
        snap_ring.step()
    (first, new_cov) = gate_all([total, snap_ring], [first, new_cov])

    snap_ring.step()
    snap_ring.pass_on_full()
    total.round()
    if end > 16:
        new_cov = fill(new_cov, range(10, end - 6))
    new_cov = fill(new_cov, [end - 6, end - 4])
    (first, new_cov) = gate_all([total, snap_ring], [first, new_cov])
    snap_ring.pass_on()
    total.round()
    new_cov = fill(new_cov, [end - 5, end - 3])
    (first, new_cov) = gate_all([total, snap_ring], [first, new_cov])
    while total.rounds:
        total.round()
    new_cov = fill(new_cov, [end - 2, end - 1])
    (first, new_cov) = gate_all([total], [first, new_cov])
    theirs = lax.ppermute(total.mine, "row", swap)
    factors = both_factors(line, bits, total.mine, theirs, first)
    new_basis = finish(line, factors, applied)
    return (new_cov, new_basis)


def solution(mesh):
    return jax.shard_map(
        functools.partial(local, mesh.shape["row"]),
        mesh=mesh,
        in_specs=(
            P(("band", "row"), None),
            P(None, ("band", "row"), None),
            P(("band", "row"), None),
        ),
        out_specs=(P(("band", "row"), None), P(("band", "row"), None)),
        check_vma=False,
    )
```

```python
import functools

import jax
import jax.numpy as jnp
import numpy as np
from jax import lax
from jax.experimental import pallas as pl
from jax.experimental.pallas import tpu as pltpu
from jax.sharding import PartitionSpec as P

forget_factor = 0.9
code_span = 240.0
code_middle = 120.0
scale_rows = 16
ln2 = 0.6931471805599453
in_vmem = pl.BlockSpec(memory_space=pltpu.VMEM)
anywhere = pl.BlockSpec(memory_space=pl.ANY)
in_hbm = pl.BlockSpec(memory_space=pltpu.HBM)
in_smem = pl.BlockSpec(memory_space=pltpu.SMEM)
params = pltpu.CompilerParams(vmem_limit_bytes=16 * 2**20)

inner = (((1,), (0,)), ((), ()))
lead = (((0,), (0,)), ((), ()))
trail = (((1,), (1,)), ((), ()))


def dot(a, b, dims):
    return lax.dot_general(a, b, dims, preferred_element_type=jnp.float32)


def split(x):
    high = x.astype(jnp.bfloat16)
    return high, (x - high.astype(jnp.float32)).astype(jnp.bfloat16)


def dot3(a, b, dims):
    a_high, a_low = split(a)
    b_high, b_low = split(b)
    return dot(a_high, b_high, dims) + (dot(a_high, b_low, dims) + dot(a_low, b_high, dims))


def dot2(a, b, dims):
    b_high, b_low = split(b)
    return dot(a, b_high, dims) + dot(a, b_low, dims)


def gate(values, events=()):
    count = len(values)

    def kernel(*refs):
        pass

    return list(
        pl.pallas_call(
            kernel,
            out_shape=tuple(jax.ShapeDtypeStruct(v.shape, v.dtype) for v in values),
            in_specs=[anywhere] * (count + len(events)),
            out_specs=(anywhere,) * count,
            input_output_aliases={i: i for i in range(count)},
            compiler_params=params,
            name="gate",
        )(*values, *events)
    )


def ring_order(devices):
    chips = devices // 2
    return list(range(0, chips, 2)) + list(range(chips - 1, 0, -2))


def ring_pairs(devices, stream):
    order = ring_order(devices)
    chips = len(order)
    pairs = []
    for at in range(chips):
        for core in range(2):
            way = 1 if core == stream else -1
            pairs.append((2 * order[at] + core, 2 * order[(at + way) % chips] + core))
    return pairs


def partner_pairs(devices, mask):
    return [(i, i ^ mask) for i in range(devices)]


def ring_table(devices, rows):
    order = ring_order(devices)
    chips = len(order)
    table = []
    for me in range(devices):
        at, core = order.index(me // 2), me % 2
        line = [me * rows, (me ^ 1) * rows]
        for step in range(1, chips // 2):
            for stream in range(2):
                way = 1 if core == stream else -1
                mine = order[(at - way * step) % chips]
                theirs = order[(at + way * step) % chips]
                line += [(2 * mine + core) * rows, (2 * theirs + 1 - core) * rows]
        chip = order[(at + chips // 2) % chips]
        line += [(2 * chip + core) * rows, (2 * chip + 1 - core) * rows]
        line += [core, (me // 2) % 2]
        table.append(line)
    return np.array(table, np.int32)


class Ring:
    def __init__(self, block, devices):
        self.streams = [ring_pairs(devices, stream) for stream in range(2)]
        self.swap = partner_pairs(devices, 1)
        self.steps = devices // 4
        self.done = 0
        self.recent = [block]
        self.groups = []
        self.new_recent = self.new_swapped = False

    def pass_on(self, copies=None):
        group = []
        for block, copy in zip(self.recent, copies or self.recent):
            group += [block, lax.ppermute(copy, "row", self.swap)]
        self.groups.append(group)
        self.new_swapped = True

    def pass_on_full(self, copies=None):
        arrived, self.recent = self.recent, self.full
        self.pass_on(copies)
        self.recent = arrived

    def step(self):
        self.done += 1
        self.new_recent = True
        self.full = self.recent
        sent = self.recent if len(self.recent) == 2 else self.recent * 2
        last = self.done == self.steps
        streams = self.streams[:1] if last else self.streams
        self.recent = [lax.ppermute(b, "row", pairs) for b, pairs in zip(sent, streams)]

    def held(self):
        return (self.recent if self.new_recent else []) + (
            self.groups[-1][1::2] if self.new_swapped else []
        )

    def hold(self, values):
        values = list(values)
        if self.new_recent:
            old, count = self.recent, len(self.recent)
            self.recent, values = values[:count], values[count:]
            for group in self.groups:
                for at, block in enumerate(group):
                    for before, now in zip(old, self.recent):
                        if block is before:
                            group[at] = now
        if self.new_swapped:
            self.groups[-1][1::2] = values
        self.new_recent = self.new_swapped = False


def small_kernel(kernel, out_shape, args, name):
    multiple = isinstance(out_shape, tuple)
    return pl.pallas_call(
        kernel,
        out_shape=out_shape,
        in_specs=[in_smem] + [in_vmem] * (len(args) - 1),
        out_specs=tuple(in_vmem for _ in out_shape) if multiple else in_vmem,
        compiler_params=params,
        name=name,
    )(*args)


def f32(*shape):
    return jax.ShapeDtypeStruct(shape, jnp.float32)


def store_halves(line_ref, bit, value_ref, mine_ref, theirs_ref):
    half = mine_ref.shape[0]
    side = line_ref[0, bit]
    mine_ref[...] = value_ref[pl.ds(pl.multiple_of(side * half, 8), half), :]
    theirs_ref[...] = value_ref[pl.ds(pl.multiple_of((1 - side) * half, 8), half), :]


def add_all(line, values):
    def kernel(line_ref, *refs):
        total = refs[0][...]
        for ref in refs[1:-1]:
            total = total + ref[...]
        refs[-1][...] = total

    return small_kernel(kernel, f32(*values[0].shape), (line, *values), "add_all")


def add_and_halve(line, bit, a, b):
    half = f32(a.shape[0] // 2, a.shape[1])

    def kernel(line_ref, a_ref, b_ref, mine_ref, theirs_ref):
        size = mine_ref.shape[0]
        side = line_ref[0, bit]
        for out_ref, which in ((mine_ref, side), (theirs_ref, 1 - side)):
            rows = pl.ds(pl.multiple_of(which * size, 8), size)
            out_ref[...] = a_ref[rows, :] + b_ref[rows, :]

    return small_kernel(kernel, (half, half), (line, a, b), "add_and_halve")


def join_halves(line, bit, mine, theirs):
    def kernel(line_ref, mine_ref, theirs_ref, out_ref):
        size = mine_ref.shape[0]
        side = line_ref[0, bit]
        out_ref[pl.ds(pl.multiple_of(side * size, 8), size), :] = mine_ref[...]
        out_ref[pl.ds(pl.multiple_of((1 - side) * size, 8), size), :] = theirs_ref[...]

    shape = f32(2 * mine.shape[0], mine.shape[1])
    return small_kernel(kernel, shape, (line, mine, theirs), "join_halves")


class Total:
    def __init__(self, line, bits, mine, theirs, devices, halve_chips):
        self.line, self.bits, self.devices = line, bits, devices
        self.mine, self.theirs = mine, theirs
        first = 4 if halve_chips else 2
        self.rounds = ["core"] + ["halve"] * halve_chips
        while first < devices:
            self.rounds.append(first)
            first *= 2
        self.rounds += ["join"] * halve_chips + ["last"]

    def pass_on(self, value, mask):
        return lax.ppermute(value, "row", partner_pairs(self.devices, mask))

    def round(self, count=1):
        for _ in range(count):
            if not self.rounds:
                return
            kind = self.rounds.pop(0)
            line, (core_bit, chip_bit) = self.line, self.bits
            if kind == "core":
                got = self.pass_on(self.theirs, 1)
                if self.rounds[0] == "halve":
                    self.mine, self.theirs = add_and_halve(line, chip_bit, self.mine, got)
                else:
                    self.mine, self.theirs = add_all(line, [self.mine, got]), None
            elif kind == "halve":
                self.mine = add_all(line, [self.mine, self.pass_on(self.theirs, 2)])
                self.theirs = None
            elif kind == "join":
                self.mine = join_halves(line, chip_bit, self.mine, self.pass_on(self.mine, 2))
            elif kind == "last":
                self.mine = join_halves(line, core_bit, self.mine, self.pass_on(self.mine, 1))
            else:
                self.mine = add_all(line, [self.mine, self.pass_on(self.mine, kind)])

    def held(self):
        return [self.mine] if self.theirs is None else [self.mine, self.theirs]

    def hold(self, values):
        self.mine = values[0]
        if self.theirs is not None:
            self.theirs = values[1]


def gate_all(parts, extra=(), events=()):
    lists = [p.held() for p in parts]
    flat = [v for values in lists for v in values] + list(extra)
    flat = gate(flat, events)
    at = 0
    for p, values in zip(parts, lists):
        p.hold(flat[at : at + len(values)])
        at += len(values)
    return flat[at:]


def encode(values):
    size = jnp.abs(values)
    most = jnp.max(size, axis=0, keepdims=True)
    level = size / jnp.maximum(most, 1e-37)
    power = jnp.exp((level * code_span - code_middle) * ln2)
    return jnp.where(values < 0.0, -power, power).astype(jnp.bfloat16), most


def decode(code, most):
    code = code.astype(jnp.float32)
    level = (jnp.log(jnp.abs(code)) * (1.0 / ln2) + code_middle) * (1.0 / code_span)
    return jnp.where(code < 0.0, -level, level) * most


def write_rows(rows):
    at = lax.broadcasted_iota(jnp.int32, (scale_rows, rows[0].shape[1]), 0)
    block = jnp.zeros(at.shape, jnp.float32)
    for i, row in enumerate(rows):
        high = row.astype(jnp.bfloat16).astype(jnp.float32)
        block = jnp.where(at == 2 * i, high, block)
        block = jnp.where(at == 2 * i + 1, row - high, block)
    return block.astype(jnp.bfloat16)


def read_row(block, i):
    block = block.astype(jnp.float32)
    return block[2 * i : 2 * i + 1] + block[2 * i + 1 : 2 * i + 2]


def pack(line, values, mine, got, extra):
    rows, rank = values.shape
    sum_rows = mine.shape[0]
    size = rows + scale_rows + sum_rows
    more = [] if extra is None else [extra]

    def kernel(line_ref, values_ref, mine_ref, got_ref, *refs):
        out_ref = refs[-1]
        code, most = encode(values_ref[...])
        sum_code, sum_most = encode(mine_ref[...] + got_ref[...])
        scales = [most, sum_most] + ([refs[0][:1, :]] if more else [])
        out_ref[:rows, :] = code
        out_ref[rows : rows + scale_rows, :] = write_rows(scales)
        out_ref[rows + scale_rows :, :] = sum_code

    return small_kernel(
        kernel,
        jax.ShapeDtypeStruct((size, rank), jnp.bfloat16),
        (line, values, mine, got, *more),
        "pack",
    )


def first_sums(line, bits, snapshots, basis):
    _, _, count = snapshots.shape
    rank = basis.shape[1]
    half = f32(count // 2, rank)

    def kernel(
        line_ref, snap_ref, basis_ref, mine_ref, theirs_ref, snap_copy_ref, basis_copy_ref, part
    ):
        part[...] = dot2(snap_ref[0], basis_ref[...], lead)
        store_halves(line_ref, bits[0], part, mine_ref, theirs_ref)
        snap_copy_ref[...] = snap_ref[...]
        basis_copy_ref[...] = basis_ref[...]

    return pl.pallas_call(
        kernel,
        out_shape=(
            half,
            half,
            jax.ShapeDtypeStruct(snapshots.shape, snapshots.dtype),
            f32(*basis.shape),
        ),
        in_specs=[in_smem, in_vmem, in_vmem],
        out_specs=(in_vmem,) * 4,
        scratch_shapes=[pltpu.VMEM((count, rank), jnp.float32)],
        compiler_params=params,
        name="first_sums",
    )(line, snapshots, basis)


def local_trace(line, prior_cov, snapshots, event):
    windows, rows, count = snapshots.shape

    def total(x):
        return jnp.sum(jnp.sum(x, axis=0, keepdims=True), axis=1, keepdims=True)

    def kernel(line_ref, cov_ref, snap_ref, event_ref, out_ref, copy_ref):
        copy_ref[...] = snap_ref[...]
        row_at = lax.broadcasted_iota(jnp.int32, (128, 128), 0)
        col_at = lax.broadcasted_iota(jnp.int32, (128, 128), 1)
        diagonal = jnp.zeros((128, 128), jnp.float32)
        for at in range(0, rows, 128):
            first = pl.multiple_of(line_ref[0, 0] + at, 128)
            corner = cov_ref[at : at + 128, pl.ds(first, 128)]
            diagonal = diagonal + jnp.where(row_at == col_at, corner, 0.0)
        prior = total(diagonal)
        trace = prior
        for w in range(windows):
            snap = snap_ref[w].astype(jnp.float32)
            trace = forget_factor * trace + total(snap * snap) * (1.0 / count)
        at = lax.broadcasted_iota(jnp.int32, out_ref.shape, 0)
        out_ref[...] = jnp.where(at == 0, trace, prior * (1.0 / rows))

    shapes = (f32(8, 128), jax.ShapeDtypeStruct(snapshots.shape, snapshots.dtype))
    return small_kernel(kernel, shapes, (line, prior_cov, snapshots, event), "local_trace")


def add_products(line_ref, base, cov_ref, block_refs, state, mean):
    running, own, other = state[:3]
    rows, rank = running.shape
    for at, block_ref in enumerate(block_refs):
        first = pl.multiple_of(line_ref[0, base + at], 128)
        scales = block_ref[rows : rows + scale_rows, :]
        block = decode(block_ref[:rows, :], read_row(scales, 0))
        piece = decode(block_ref[rows + scale_rows :, :], read_row(scales, 1))
        if at % 2 == 0:
            own = own + piece
        else:
            other = other + piece
        high, low = split(block)
        if mean is not None:
            gram, trace = state[3:]
            both = jnp.concatenate([high, low], axis=1)
            square = dot(high, both, lead)
            gram = gram + (square[:, :rank] + (square[:, rank:] + dot(low, high, lead)))
            trace = trace + read_row(scales, 2)
            state = (running, own, other, gram, trace)
            high, low = split(block * (1.0 / mean))
        both = jnp.concatenate([high, low], axis=1)
        cov_high, cov_low = split(cov_ref[:, pl.ds(first, rows)])
        wide = dot(cov_high, both, inner)
        running = running + (wide[:, :rank] + (wide[:, rank:] + dot(cov_low, high, inner)))
    return (running, own, other) + tuple(state[3:])


def state_shapes(rows, rank, sum_rows, last):
    shapes = [f32(n, rank) for n in (rows, sum_rows, sum_rows)]
    return shapes + ([f32(rank, rank), f32(1, rank)] if last else [])


def product_part(line, base, prior_cov, blocks, state, sum_rows, share, carried):
    count = len(blocks)
    last = share is not None
    shapes = state_shapes(prior_cov.shape[0], blocks[0].shape[1], sum_rows, last)
    outs = len(shapes)
    shapes += [jax.ShapeDtypeStruct(v.shape, v.dtype) for v in carried]
    more = ([share] if last else []) + list(state or [])

    def kernel(line_ref, cov_ref, *refs):
        block_refs, refs = refs[:count], refs[count:]
        carried_refs, refs = refs[: len(carried)], refs[len(carried) :]
        given, out_refs = refs[: -len(shapes)], refs[-len(shapes) :]
        for carried_ref, out_ref in zip(carried_refs, out_refs[outs:]):
            out_ref[...] = carried_ref[...]
        mean = None
        if last:
            mean, given = given[0][1:2, :1], given[1:]
        old = [r[...] for r in given] or [jnp.zeros(v.shape, jnp.float32) for v in shapes[:outs]]
        new = add_products(line_ref, base, cov_ref, block_refs, tuple(old), mean)
        for out_ref, value in zip(out_refs[:outs], new):
            out_ref[...] = value

    results = small_kernel(
        kernel, tuple(shapes), (line, prior_cov, *blocks, *carried, *more), "product_part"
    )
    return list(results[:outs]), list(results[outs:])


def product_end(line, bits, base, prior_cov, blocks, state, snapshots, window, share):
    rows, order = prior_cov.shape
    rank = blocks[0].shape[1]
    windows, _, snap_count = snapshots.shape
    count = len(blocks)
    last = share is not None
    sum_rows = state[1].shape[0]
    inv_snap = 1.0 / snap_count
    parts = len(state)
    more = [share] if last else []
    shapes = (f32(rows, rank),)
    if last:
        shapes += (f32(rank // 2, rank), f32(rank // 2, rank), f32(rank, rank))

    def kernel(line_ref, cov_ref, *refs):
        block_refs, refs = refs[:count], refs[count:]
        old = tuple(r[...] for r in refs[:parts])
        snap_ref, refs = refs[parts], refs[parts + 1 :]
        mean = None
        if last:
            mean, refs = refs[0][1:2, :1], refs[1:]
        outs, sums_buf, gram_buf = refs[: len(shapes)], refs[-2], refs[-1]
        new = add_products(line_ref, base, cov_ref, block_refs, old, mean)
        side = line_ref[0, bits[0]]
        sums_buf[pl.ds(pl.multiple_of(side * sum_rows, 8), sum_rows), :] = new[1]
        sums_buf[pl.ds(pl.multiple_of((1 - side) * sum_rows, 8), sum_rows), :] = new[2]
        applied = new[0] * forget_factor ** (window + 1)
        scale = 1.0
        if last:
            scale = float(order) / new[4]
            applied = applied * (scale * mean)
        for w in range(window + 1):
            at = w * snap_count
            total = sums_buf[at : at + snap_count, :] * scale
            weight = forget_factor ** (window - w) * inv_snap
            applied = applied + weight * dot2(snap_ref[w], total, inner)
        outs[0][...] = applied
        if last:
            gram_buf[...] = lax.dot_general(
                applied,
                applied,
                lead,
                precision=lax.Precision.HIGHEST,
                preferred_element_type=jnp.float32,
            )
            store_halves(line_ref, bits[0], gram_buf, outs[1], outs[2])
            outs[3][...] = new[3]

    return pl.pallas_call(
        kernel,
        out_shape=shapes,
        in_specs=[in_smem] + [in_vmem] * (2 + count + parts + len(more)),
        out_specs=tuple(in_vmem for _ in shapes),
        scratch_shapes=[
            pltpu.VMEM((2 * sum_rows, rank), jnp.float32),
            pltpu.VMEM((rank, rank), jnp.float32),
        ],
        compiler_params=params,
        name="product_end",
    )(line, prior_cov, *blocks, *state, snapshots, *more)


def window_sums(line, bits, applied, snapshots):
    windows, _, snap_count = snapshots.shape
    rank = applied.shape[1]
    total = windows * snap_count
    half = f32(total // 2, rank)

    def kernel(line_ref, applied_ref, snap_ref, mine_ref, theirs_ref, part):
        for w in range(windows):
            at = w * snap_count
            part[at : at + snap_count, :] = dot2(snap_ref[w], applied_ref[...], lead)
        store_halves(line_ref, bits[0], part, mine_ref, theirs_ref)

    return pl.pallas_call(
        kernel,
        out_shape=(half, half),
        in_specs=[in_smem] + [in_vmem] * 2,
        out_specs=(in_vmem, in_vmem),
        scratch_shapes=[pltpu.VMEM((total, rank), jnp.float32)],
        compiler_params=params,
        name="window_sums",
    )(line, applied, snapshots)


panel = 8


def reciprocal(x):
    guess = pl.reciprocal(x, approx=True)
    guess = guess * (2.0 - x * guess)
    return guess * (2.0 - x * guess)


def inverse_factor(gram):
    rank = gram.shape[0]
    eye = lax.broadcasted_iota(jnp.int32, (rank, rank), 0) == lax.broadcasted_iota(
        jnp.int32, (rank, rank), 1
    )
    diagonal = jnp.where(eye, gram, 0.0)
    down = lax.rsqrt(jnp.sum(diagonal, axis=1, keepdims=True))
    along = lax.rsqrt(jnp.sum(diagonal, axis=0, keepdims=True))
    gram = gram * down * along
    start = jnp.where(eye, along, 0.0)
    count = rank // panel
    rows = [gram[i * panel : (i + 1) * panel] for i in range(count)]
    sides = [start[i * panel : (i + 1) * panel] for i in range(count)]
    sub = lax.broadcasted_iota(jnp.int32, (panel, rank), 0)
    finished = []
    for top in range(count):
        first = top * panel
        spread = {
            i: [
                jnp.broadcast_to(rows[i][:, first + k : first + k + 1], (panel, rank))
                for k in range(panel)
            ]
            for i in range(top, count)
        }
        done = jnp.zeros((panel, rank), jnp.float32)
        for j in range(0, panel, 2):
            row0, row1 = rows[top][j : j + 1], rows[top][j + 1 : j + 2]
            side0, side1 = sides[top][j : j + 1], sides[top][j + 1 : j + 2]
            lead_columns = spread[top]
            a = lead_columns[j][j : j + 1]
            b = lead_columns[j][j + 1 : j + 2]
            c = lead_columns[j + 1][j + 1 : j + 2]
            over = reciprocal(a * c - b * b)
            a_over, b_over, c_over = a * over, b * over, c * over
            root = lax.rsqrt(a)
            ratio = b * root * root
            done = jnp.where(sub == j, side0 * root, done)
            done = jnp.where(
                sub == j + 1, (side1 - ratio * side0) * lax.rsqrt(c - ratio * b), done
            )
            heads = [
                (lead_columns[m][j : j + 1], lead_columns[m][j + 1 : j + 2]) for m in range(panel)
            ]
            for i in range(top, count):
                x0, x1 = spread[i][j], spread[i][j + 1]
                m0 = x0 * c_over - x1 * b_over
                m1 = x1 * a_over - x0 * b_over
                rows[i] = rows[i] - (m0 * row0 + m1 * row1)
                sides[i] = sides[i] - (m0 * side0 + m1 * side1)
                for m in range(j + 2, panel):
                    head0, head1 = heads[m]
                    spread[i][m] = spread[i][m] - (m0 * head0 + m1 * head1)
        finished.append(done)
    return jnp.concatenate(finished, axis=0)


def factor(line, gram):
    def kernel(line_ref, gram_ref, out_ref):
        out_ref[...] = inverse_factor(gram_ref[...])

    return small_kernel(kernel, f32(*gram.shape), (line, gram), "factor")


def both_factors(line, bits, gram, theirs, first):
    rank = gram.shape[1]
    half = rank // 2

    def exact(a, b, dims):
        return lax.dot_general(
            a, b, dims, precision=lax.Precision.HIGHEST, preferred_element_type=jnp.float32
        )

    def kernel(line_ref, gram_ref, theirs_ref, first_ref, out_ref, buf):
        side = line_ref[0, bits[0]]
        buf[pl.ds(pl.multiple_of(side * half, 8), half), :] = gram_ref[...]
        buf[pl.ds(pl.multiple_of((1 - side) * half, 8), half), :] = theirs_ref[...]
        first = first_ref[...]
        second_gram = exact(exact(first, buf[...], inner), first, trail)
        out_ref[...] = exact(inverse_factor(second_gram), first, inner)

    return pl.pallas_call(
        kernel,
        out_shape=f32(rank, rank),
        in_specs=[in_smem] + [in_vmem] * 3,
        out_specs=in_vmem,
        scratch_shapes=[pltpu.VMEM((rank, rank), jnp.float32)],
        compiler_params=params,
        name="both_factors",
    )(line, gram, theirs, first)


def finish(line, factors, applied):
    def kernel(line_ref, factors_ref, applied_ref, out_ref):
        out_ref[...] = dot3(applied_ref[...], factors_ref[...], trail)

    return small_kernel(kernel, f32(*applied.shape), (line, factors, applied), "finish")


def covariance_part(line, numbers, prior_cov, snapshots, blocks, filled, carry=False):
    rows, _ = prior_cov.shape
    windows, _, snap_count = snapshots.shape
    count = len(blocks)
    more = [] if filled is None else [filled]
    copied = count if carry else 0
    inv_snap = 1.0 / snap_count

    def kernel(line_ref, cov_ref, snap_ref, *refs):
        block_refs, refs = refs[:count], refs[count + len(more) :]
        out_ref, copy_refs, refs = refs[0], refs[1 : 1 + copied], refs[1 + copied :]
        out_bufs, sems = refs[:-1], refs[-1]
        for block_ref, copy_ref in zip(block_refs, copy_refs):
            copy_ref[...] = block_ref[...]
        copies = []
        for at in range(count):
            width = block_refs[at].shape[1]
            first = pl.multiple_of(line_ref[0, numbers[at]], 128)
            columns = pl.ds(first, width)
            total = cov_ref[:, columns] * forget_factor**windows
            for w in range(windows):
                weight = forget_factor ** (windows - 1 - w) * inv_snap
                total = total + weight * dot(snap_ref[w], block_refs[at][w], trail)
            out_bufs[at][...] = total
            copy = pltpu.make_async_copy(out_bufs[at], out_ref.at[:, columns], sems.at[at])
            copy.start()
            copies.append(copy)
        for copy in copies:
            copy.wait()

    result = pl.pallas_call(
        kernel,
        out_shape=(f32(*prior_cov.shape),)
        + tuple(jax.ShapeDtypeStruct(b.shape, b.dtype) for b in blocks[:copied]),
        in_specs=[in_smem] + [in_vmem] * (2 + count) + [in_hbm] * len(more),
        out_specs=(in_hbm,) + (in_vmem,) * copied,
        scratch_shapes=[pltpu.VMEM((rows, b.shape[1]), jnp.float32) for b in blocks]
        + [pltpu.SemaphoreType.DMA((count,))],
        input_output_aliases={3 + count: 0} if more else {},
        compiler_params=params,
        name="covariance_part",
    )(line, prior_cov, snapshots, *blocks, *more)
    return (result[0], list(result[1:])) if carry else result[0]


def local(devices, prior_cov, snapshots, prior_basis):
    rows = prior_cov.shape[0]
    rank = prior_basis.shape[1]
    windows, _, snap_count = snapshots.shape
    table = ring_table(devices, rows)
    me = lax.axis_index("row")
    line = lax.dynamic_slice_in_dim(jnp.asarray(table), me, 1, axis=0)
    entries = table.shape[1]
    bits = (entries - 2, entries - 1)
    steps = devices // 4
    starts = [0] + [2 + 4 * at for at in range(steps)]
    swap = partner_pairs(devices, 1)

    def fill(filled, numbers):
        blocks = [b for group in snap_ring.groups for b in group]
        chosen = [blocks[n] for n in numbers]
        return covariance_part(line, numbers, prior_cov, snapshots, chosen, filled)

    def fill_own(filled, blocks, numbers):
        return covariance_part(line, numbers, prior_cov, snapshots, blocks, filled, True)

    end = 4 * steps
    snap_ring = Ring(snapshots, devices)
    snap_ring.step()
    mine, theirs, snapshots, values = first_sums(line, bits, snapshots, prior_basis)
    share = new_cov = None
    for window in range(windows):
        got = lax.ppermute(theirs, "row", swap)
        if window == 1:
            (values,) = gate_all([snap_ring], [values])
        ring = Ring(pack(line, values, mine, got, share), devices)
        sum_rows = mine.shape[0]
        state = None
        for phase in range(1, steps + 1):
            if phase == steps:
                ready = state[0]
            sent = ring.recent
            ring.step()
            arrived, ring.recent = ring.recent, sent
            ring.pass_on()
            extra, waiting, filled = [], [ring], []
            if phase == 1:
                waiting.append(snap_ring)
                if window == 0:
                    next_share, snap_copy = local_trace(line, prior_cov, snapshots, sent[0])
                    arrived = gate(arrived, [next_share])
                    extra = [snap_copy]
                else:
                    snap_ring.recent = gate(snap_ring.recent, [sent[0]])
                    snap_ring.pass_on()
                    arrived = gate(arrived)
                    filled = [3, 5, 6, 8]
            else:
                state, _ = product_part(
                    line,
                    starts[phase - 2],
                    prior_cov,
                    ring.groups[phase - 2],
                    state,
                    sum_rows,
                    share,
                    [],
                )
                arrived = gate(arrived, [state[0]])
                extra += state
                if window == 0 and phase == 2:
                    snap_ring.full = [snap_copy]
                    snap_ring.pass_on_full()
                    snap_ring.groups[0][0] = snapshots
                    waiting.append(snap_ring)
                if window == 0 and phase == 3:
                    filled = [0, 1]
                if window == 1 and phase == 2:
                    filled = [7, 9]
            if filled:
                new_cov = fill(new_cov, filled)
                extra.append(new_cov)
            ring.recent = arrived
            if phase == steps and window == 1:
                snap_ring.new_recent = True
                waiting.append(snap_ring)
            if phase == steps and window == 0:
                snap_ring.recent = gate(snap_ring.recent, [ready])
                snap_ring.step()
                if window == 0:
                    new_cov, copies = fill_own(new_cov, snap_ring.full, [2, 4])
                    extra += copies + [new_cov]
                    filled = [2, 4]
            extra = gate_all(waiting, extra)
            if window == 0 and phase == 1:
                snap_copy = extra.pop()
            if filled:
                new_cov = extra.pop()
            if window == 0 and phase == steps:
                extra, copies = extra[:-2], extra[-2:]
            state = extra or None
        if window == 0:
            snap_ring.pass_on_full(copies)
        else:
            snap_ring.step()
        state, _ = product_part(
            line,
            starts[steps - 1],
            prior_cov,
            ring.groups[steps - 1],
            state,
            sum_rows,
            share,
            [],
        )
        ring.pass_on()
        result = product_end(
            line,
            bits,
            starts[steps],
            prior_cov,
            ring.groups[steps],
            state,
            snapshots,
            window,
            share,
        )
        if window == 0:
            (values,) = result
            share = next_share
            mine, theirs = window_sums(line, bits, values, snapshots)
    applied, mine, theirs, first_gram = result
    total = Total(line, bits, mine, theirs, devices, False)
    total.rounds.pop()
    total.round()
    first = factor(line, first_gram)
    while snap_ring.done < steps - 1:
        (first,) = gate_all([total, snap_ring], [first])
        snap_ring.pass_on()
        snap_ring.step()
    (first, new_cov) = gate_all([total, snap_ring], [first, new_cov])

    snap_ring.step()
    snap_ring.pass_on_full()
    total.round()
    if end > 16:
        new_cov = fill(new_cov, range(10, end - 6))
    new_cov = fill(new_cov, [end - 6, end - 4])
    (first, new_cov) = gate_all([total, snap_ring], [first, new_cov])
    snap_ring.pass_on()
    total.round()
    new_cov = fill(new_cov, [end - 5, end - 3])
    (first, new_cov) = gate_all([total, snap_ring], [first, new_cov])
    while total.rounds:
        total.round()
    new_cov = fill(new_cov, [end - 2, end - 1])
    (first, new_cov) = gate_all([total], [first, new_cov])
    theirs = lax.ppermute(total.mine, "row", swap)
    factors = both_factors(line, bits, total.mine, theirs, first)
    new_basis = finish(line, factors, applied)
    return (new_cov, new_basis)


def solution(mesh):
    return jax.shard_map(
        functools.partial(local, mesh.shape["row"]),
        mesh=mesh,
        in_specs=(
            P(("band", "row"), None),
            P(None, ("band", "row"), None),
            P(("band", "row"), None),
        ),
        out_specs=(P(("band", "row"), None), P(("band", "row"), None)),
        check_vma=False,
    )
```

```python
import functools

import jax
import jax.numpy as jnp
import numpy as np
from jax import lax
from jax.experimental import pallas as pl
from jax.experimental.pallas import tpu as pltpu
from jax.sharding import PartitionSpec as P

forget_factor = 0.9
code_span = 240.0
code_middle = 120.0
scale_rows = 16
ln2 = 0.6931471805599453
in_vmem = pl.BlockSpec(memory_space=pltpu.VMEM)
anywhere = pl.BlockSpec(memory_space=pl.ANY)
in_hbm = pl.BlockSpec(memory_space=pltpu.HBM)
in_smem = pl.BlockSpec(memory_space=pltpu.SMEM)
params = pltpu.CompilerParams(vmem_limit_bytes=16 * 2**20)

inner = (((1,), (0,)), ((), ()))
lead = (((0,), (0,)), ((), ()))
trail = (((1,), (1,)), ((), ()))


def dot(a, b, dims):
    return lax.dot_general(a, b, dims, preferred_element_type=jnp.float32)


def split(x):
    high = x.astype(jnp.bfloat16)
    return high, (x - high.astype(jnp.float32)).astype(jnp.bfloat16)


def dot3(a, b, dims):
    a_high, a_low = split(a)
    b_high, b_low = split(b)
    return dot(a_high, b_high, dims) + (dot(a_high, b_low, dims) + dot(a_low, b_high, dims))


def dot2(a, b, dims):
    b_high, b_low = split(b)
    return dot(a, b_high, dims) + dot(a, b_low, dims)


def gate(values, events=()):
    count = len(values)

    def kernel(*refs):
        pass

    return list(
        pl.pallas_call(
            kernel,
            out_shape=tuple(jax.ShapeDtypeStruct(v.shape, v.dtype) for v in values),
            in_specs=[anywhere] * (count + len(events)),
            out_specs=(anywhere,) * count,
            input_output_aliases={i: i for i in range(count)},
            compiler_params=params,
            name="gate",
        )(*values, *events)
    )


def ring_order(devices):
    chips = devices // 2
    return list(range(0, chips, 2)) + list(range(chips - 1, 0, -2))


def ring_pairs(devices, stream):
    order = ring_order(devices)
    chips = len(order)
    pairs = []
    for at in range(chips):
        for core in range(2):
            way = 1 if core == stream else -1
            pairs.append((2 * order[at] + core, 2 * order[(at + way) % chips] + core))
    return pairs


def partner_pairs(devices, mask):
    return [(i, i ^ mask) for i in range(devices)]


def ring_table(devices, rows):
    order = ring_order(devices)
    chips = len(order)
    table = []
    for me in range(devices):
        at, core = order.index(me // 2), me % 2
        line = [me * rows, (me ^ 1) * rows]
        for step in range(1, chips // 2):
            for stream in range(2):
                way = 1 if core == stream else -1
                mine = order[(at - way * step) % chips]
                theirs = order[(at + way * step) % chips]
                line += [(2 * mine + core) * rows, (2 * theirs + 1 - core) * rows]
        chip = order[(at + chips // 2) % chips]
        line += [(2 * chip + core) * rows, (2 * chip + 1 - core) * rows]
        line += [core, (me // 2) % 2]
        table.append(line)
    return np.array(table, np.int32)


class Ring:
    def __init__(self, block, devices):
        self.streams = [ring_pairs(devices, stream) for stream in range(2)]
        self.swap = partner_pairs(devices, 1)
        self.steps = devices // 4
        self.done = 0
        self.recent = [block]
        self.groups = []
        self.new_recent = self.new_swapped = False

    def pass_on(self, copies=None):
        group = []
        for block, copy in zip(self.recent, copies or self.recent):
            group += [block, lax.ppermute(copy, "row", self.swap)]
        self.groups.append(group)
        self.new_swapped = True

    def pass_on_full(self, copies=None):
        arrived, self.recent = self.recent, self.full
        self.pass_on(copies)
        self.recent = arrived

    def step(self):
        self.done += 1
        self.new_recent = True
        self.full = self.recent
        sent = self.recent if len(self.recent) == 2 else self.recent * 2
        last = self.done == self.steps
        streams = self.streams[:1] if last else self.streams
        self.recent = [lax.ppermute(b, "row", pairs) for b, pairs in zip(sent, streams)]

    def held(self):
        return (self.recent if self.new_recent else []) + (
            self.groups[-1][1::2] if self.new_swapped else []
        )

    def hold(self, values):
        values = list(values)
        if self.new_recent:
            old, count = self.recent, len(self.recent)
            self.recent, values = values[:count], values[count:]
            for group in self.groups:
                for at, block in enumerate(group):
                    for before, now in zip(old, self.recent):
                        if block is before:
                            group[at] = now
        if self.new_swapped:
            self.groups[-1][1::2] = values
        self.new_recent = self.new_swapped = False


def small_kernel(kernel, out_shape, args, name):
    multiple = isinstance(out_shape, tuple)
    return pl.pallas_call(
        kernel,
        out_shape=out_shape,
        in_specs=[in_smem] + [in_vmem] * (len(args) - 1),
        out_specs=tuple(in_vmem for _ in out_shape) if multiple else in_vmem,
        compiler_params=params,
        name=name,
    )(*args)


def f32(*shape):
    return jax.ShapeDtypeStruct(shape, jnp.float32)


def store_halves(line_ref, bit, value_ref, mine_ref, theirs_ref):
    half = mine_ref.shape[0]
    side = line_ref[0, bit]
    mine_ref[...] = value_ref[pl.ds(pl.multiple_of(side * half, 8), half), :]
    theirs_ref[...] = value_ref[pl.ds(pl.multiple_of((1 - side) * half, 8), half), :]


def add_all(line, values):
    def kernel(line_ref, *refs):
        total = refs[0][...]
        for ref in refs[1:-1]:
            total = total + ref[...]
        refs[-1][...] = total

    return small_kernel(kernel, f32(*values[0].shape), (line, *values), "add_all")


def add_and_halve(line, bit, a, b):
    half = f32(a.shape[0] // 2, a.shape[1])

    def kernel(line_ref, a_ref, b_ref, mine_ref, theirs_ref):
        size = mine_ref.shape[0]
        side = line_ref[0, bit]
        for out_ref, which in ((mine_ref, side), (theirs_ref, 1 - side)):
            rows = pl.ds(pl.multiple_of(which * size, 8), size)
            out_ref[...] = a_ref[rows, :] + b_ref[rows, :]

    return small_kernel(kernel, (half, half), (line, a, b), "add_and_halve")


def join_halves(line, bit, mine, theirs):
    def kernel(line_ref, mine_ref, theirs_ref, out_ref):
        size = mine_ref.shape[0]
        side = line_ref[0, bit]
        out_ref[pl.ds(pl.multiple_of(side * size, 8), size), :] = mine_ref[...]
        out_ref[pl.ds(pl.multiple_of((1 - side) * size, 8), size), :] = theirs_ref[...]

    shape = f32(2 * mine.shape[0], mine.shape[1])
    return small_kernel(kernel, shape, (line, mine, theirs), "join_halves")


class Total:
    def __init__(self, line, bits, mine, theirs, devices, halve_chips):
        self.line, self.bits, self.devices = line, bits, devices
        self.mine, self.theirs = mine, theirs
        first = 4 if halve_chips else 2
        self.rounds = ["core"] + ["halve"] * halve_chips
        while first < devices:
            self.rounds.append(first)
            first *= 2
        self.rounds += ["join"] * halve_chips + ["last"]

    def pass_on(self, value, mask):
        return lax.ppermute(value, "row", partner_pairs(self.devices, mask))

    def round(self, count=1, event=None):
        for _ in range(count):
            if not self.rounds:
                return
            kind = self.rounds.pop(0)
            line, (core_bit, chip_bit) = self.line, self.bits
            if kind == "core":
                got = self.pass_on(self.theirs, 1)
                if self.rounds[0] == "halve":
                    self.mine, self.theirs = add_and_halve(line, chip_bit, self.mine, got)
                else:
                    self.mine, self.theirs = add_all(line, [self.mine, got]), None
            elif kind == "halve":
                self.mine = add_all(line, [self.mine, self.pass_on(self.theirs, 2)])
                self.theirs = None
            elif kind == "join":
                self.mine = join_halves(line, chip_bit, self.mine, self.pass_on(self.mine, 2))
            elif kind == "last":
                self.mine = join_halves(line, core_bit, self.mine, self.pass_on(self.mine, 1))
            else:
                got = self.pass_on(self.mine, kind)
                if event is not None:
                    (got,) = gate([got], [event])
                self.mine = add_all(line, [self.mine, got])

    def held(self):
        return [self.mine] if self.theirs is None else [self.mine, self.theirs]

    def hold(self, values):
        self.mine = values[0]
        if self.theirs is not None:
            self.theirs = values[1]


def gate_all(parts, extra=(), events=()):
    lists = [p.held() for p in parts]
    flat = [v for values in lists for v in values] + list(extra)
    flat = gate(flat, events)
    at = 0
    for p, values in zip(parts, lists):
        p.hold(flat[at : at + len(values)])
        at += len(values)
    return flat[at:]


def encode(values):
    size = jnp.abs(values)
    most = jnp.max(size, axis=0, keepdims=True)
    level = size / jnp.maximum(most, 1e-37)
    power = jnp.exp((level * code_span - code_middle) * ln2)
    return jnp.where(values < 0.0, -power, power).astype(jnp.bfloat16), most


def decode(code, most):
    code = code.astype(jnp.float32)
    level = (jnp.log(jnp.abs(code)) * (1.0 / ln2) + code_middle) * (1.0 / code_span)
    return jnp.where(code < 0.0, -level, level) * most


def write_rows(rows):
    at = lax.broadcasted_iota(jnp.int32, (scale_rows, rows[0].shape[1]), 0)
    block = jnp.zeros(at.shape, jnp.float32)
    for i, row in enumerate(rows):
        high = row.astype(jnp.bfloat16).astype(jnp.float32)
        block = jnp.where(at == 2 * i, high, block)
        block = jnp.where(at == 2 * i + 1, row - high, block)
    return block.astype(jnp.bfloat16)


def read_row(block, i):
    block = block.astype(jnp.float32)
    return block[2 * i : 2 * i + 1] + block[2 * i + 1 : 2 * i + 2]


def pack(line, values, mine, got, extra):
    rows, rank = values.shape
    sum_rows = mine.shape[0]
    size = rows + scale_rows + sum_rows
    more = [] if extra is None else [extra]

    def kernel(line_ref, values_ref, mine_ref, got_ref, *refs):
        out_ref = refs[-1]
        code, most = encode(values_ref[...])
        sum_code, sum_most = encode(mine_ref[...] + got_ref[...])
        scales = [most, sum_most] + ([refs[0][:1, :]] if more else [])
        out_ref[:rows, :] = code
        out_ref[rows : rows + scale_rows, :] = write_rows(scales)
        out_ref[rows + scale_rows :, :] = sum_code

    return small_kernel(
        kernel,
        jax.ShapeDtypeStruct((size, rank), jnp.bfloat16),
        (line, values, mine, got, *more),
        "pack",
    )


def first_sums(line, bits, snapshots, basis):
    _, _, count = snapshots.shape
    rank = basis.shape[1]
    half = f32(count // 2, rank)

    def kernel(
        line_ref, snap_ref, basis_ref, mine_ref, theirs_ref, snap_copy_ref, basis_copy_ref, part
    ):
        part[...] = dot2(snap_ref[0], basis_ref[...], lead)
        store_halves(line_ref, bits[0], part, mine_ref, theirs_ref)
        snap_copy_ref[...] = snap_ref[...]
        basis_copy_ref[...] = basis_ref[...]

    return pl.pallas_call(
        kernel,
        out_shape=(
            half,
            half,
            jax.ShapeDtypeStruct(snapshots.shape, snapshots.dtype),
            f32(*basis.shape),
        ),
        in_specs=[in_smem, in_vmem, in_vmem],
        out_specs=(in_vmem,) * 4,
        scratch_shapes=[pltpu.VMEM((count, rank), jnp.float32)],
        compiler_params=params,
        name="first_sums",
    )(line, snapshots, basis)


def local_trace(line, prior_cov, snapshots, event):
    windows, rows, count = snapshots.shape

    def total(x):
        return jnp.sum(jnp.sum(x, axis=0, keepdims=True), axis=1, keepdims=True)

    def kernel(line_ref, cov_ref, snap_ref, event_ref, out_ref, copy_ref):
        copy_ref[...] = snap_ref[...]
        row_at = lax.broadcasted_iota(jnp.int32, (128, 128), 0)
        col_at = lax.broadcasted_iota(jnp.int32, (128, 128), 1)
        diagonal = jnp.zeros((128, 128), jnp.float32)
        for at in range(0, rows, 128):
            first = pl.multiple_of(line_ref[0, 0] + at, 128)
            corner = cov_ref[at : at + 128, pl.ds(first, 128)]
            diagonal = diagonal + jnp.where(row_at == col_at, corner, 0.0)
        prior = total(diagonal)
        trace = prior
        for w in range(windows):
            snap = snap_ref[w].astype(jnp.float32)
            trace = forget_factor * trace + total(snap * snap) * (1.0 / count)
        at = lax.broadcasted_iota(jnp.int32, out_ref.shape, 0)
        out_ref[...] = jnp.where(at == 0, trace, prior * (1.0 / rows))

    shapes = (f32(8, 128), jax.ShapeDtypeStruct(snapshots.shape, snapshots.dtype))
    return small_kernel(kernel, shapes, (line, prior_cov, snapshots, event), "local_trace")


def add_products(line_ref, base, cov_ref, block_refs, state, mean):
    running, own, other = state[:3]
    rows, rank = running.shape
    for at, block_ref in enumerate(block_refs):
        first = pl.multiple_of(line_ref[0, base + at], 128)
        scales = block_ref[rows : rows + scale_rows, :]
        block = decode(block_ref[:rows, :], read_row(scales, 0))
        piece = decode(block_ref[rows + scale_rows :, :], read_row(scales, 1))
        if at % 2 == 0:
            own = own + piece
        else:
            other = other + piece
        high, low = split(block)
        if mean is not None:
            gram, trace = state[3:]
            both = jnp.concatenate([high, low], axis=1)
            square = dot(high, both, lead)
            gram = gram + (square[:, :rank] + (square[:, rank:] + dot(low, high, lead)))
            trace = trace + read_row(scales, 2)
            state = (running, own, other, gram, trace)
            high, low = split(block * (1.0 / mean))
        both = jnp.concatenate([high, low], axis=1)
        cov_high, cov_low = split(cov_ref[:, pl.ds(first, rows)])
        wide = dot(cov_high, both, inner)
        running = running + (wide[:, :rank] + (wide[:, rank:] + dot(cov_low, high, inner)))
    return (running, own, other) + tuple(state[3:])


def state_shapes(rows, rank, sum_rows, last):
    shapes = [f32(n, rank) for n in (rows, sum_rows, sum_rows)]
    return shapes + ([f32(rank, rank), f32(1, rank)] if last else [])


def product_part(line, base, prior_cov, blocks, state, sum_rows, share, carried):
    count = len(blocks)
    last = share is not None
    shapes = state_shapes(prior_cov.shape[0], blocks[0].shape[1], sum_rows, last)
    outs = len(shapes)
    shapes += [jax.ShapeDtypeStruct(v.shape, v.dtype) for v in carried]
    more = ([share] if last else []) + list(state or [])

    def kernel(line_ref, cov_ref, *refs):
        block_refs, refs = refs[:count], refs[count:]
        carried_refs, refs = refs[: len(carried)], refs[len(carried) :]
        given, out_refs = refs[: -len(shapes)], refs[-len(shapes) :]
        for carried_ref, out_ref in zip(carried_refs, out_refs[outs:]):
            out_ref[...] = carried_ref[...]
        mean = None
        if last:
            mean, given = given[0][1:2, :1], given[1:]
        old = [r[...] for r in given] or [jnp.zeros(v.shape, jnp.float32) for v in shapes[:outs]]
        new = add_products(line_ref, base, cov_ref, block_refs, tuple(old), mean)
        for out_ref, value in zip(out_refs[:outs], new):
            out_ref[...] = value

    results = small_kernel(
        kernel, tuple(shapes), (line, prior_cov, *blocks, *carried, *more), "product_part"
    )
    return list(results[:outs]), list(results[outs:])


def product_end(line, bits, base, prior_cov, blocks, state, snapshots, window, share):
    rows, order = prior_cov.shape
    rank = blocks[0].shape[1]
    windows, _, snap_count = snapshots.shape
    count = len(blocks)
    last = share is not None
    sum_rows = state[1].shape[0]
    inv_snap = 1.0 / snap_count
    parts = len(state)
    more = [share] if last else []
    shapes = (f32(rows, rank),)
    if last:
        shapes += (f32(rank // 2, rank), f32(rank // 2, rank), f32(rank, rank))

    def kernel(line_ref, cov_ref, *refs):
        block_refs, refs = refs[:count], refs[count:]
        old = tuple(r[...] for r in refs[:parts])
        snap_ref, refs = refs[parts], refs[parts + 1 :]
        mean = None
        if last:
            mean, refs = refs[0][1:2, :1], refs[1:]
        outs, sums_buf, gram_buf = refs[: len(shapes)], refs[-2], refs[-1]
        new = add_products(line_ref, base, cov_ref, block_refs, old, mean)
        side = line_ref[0, bits[0]]
        sums_buf[pl.ds(pl.multiple_of(side * sum_rows, 8), sum_rows), :] = new[1]
        sums_buf[pl.ds(pl.multiple_of((1 - side) * sum_rows, 8), sum_rows), :] = new[2]
        applied = new[0] * forget_factor ** (window + 1)
        scale = 1.0
        if last:
            scale = float(order) / new[4]
            applied = applied * (scale * mean)
        for w in range(window + 1):
            at = w * snap_count
            total = sums_buf[at : at + snap_count, :] * scale
            weight = forget_factor ** (window - w) * inv_snap
            applied = applied + weight * dot2(snap_ref[w], total, inner)
        outs[0][...] = applied
        if last:
            gram_buf[...] = lax.dot_general(
                applied,
                applied,
                lead,
                precision=lax.Precision.HIGHEST,
                preferred_element_type=jnp.float32,
            )
            store_halves(line_ref, bits[0], gram_buf, outs[1], outs[2])
            outs[3][...] = new[3]

    return pl.pallas_call(
        kernel,
        out_shape=shapes,
        in_specs=[in_smem] + [in_vmem] * (2 + count + parts + len(more)),
        out_specs=tuple(in_vmem for _ in shapes),
        scratch_shapes=[
            pltpu.VMEM((2 * sum_rows, rank), jnp.float32),
            pltpu.VMEM((rank, rank), jnp.float32),
        ],
        compiler_params=params,
        name="product_end",
    )(line, prior_cov, *blocks, *state, snapshots, *more)


def window_sums(line, bits, applied, snapshots):
    windows, _, snap_count = snapshots.shape
    rank = applied.shape[1]
    total = windows * snap_count
    half = f32(total // 2, rank)

    def kernel(line_ref, applied_ref, snap_ref, mine_ref, theirs_ref, part):
        for w in range(windows):
            at = w * snap_count
            part[at : at + snap_count, :] = dot2(snap_ref[w], applied_ref[...], lead)
        store_halves(line_ref, bits[0], part, mine_ref, theirs_ref)

    return pl.pallas_call(
        kernel,
        out_shape=(half, half),
        in_specs=[in_smem] + [in_vmem] * 2,
        out_specs=(in_vmem, in_vmem),
        scratch_shapes=[pltpu.VMEM((total, rank), jnp.float32)],
        compiler_params=params,
        name="window_sums",
    )(line, applied, snapshots)


panel = 8


def reciprocal(x):
    guess = pl.reciprocal(x, approx=True)
    guess = guess * (2.0 - x * guess)
    return guess * (2.0 - x * guess)


def inverse_factor(gram):
    rank = gram.shape[0]
    eye = lax.broadcasted_iota(jnp.int32, (rank, rank), 0) == lax.broadcasted_iota(
        jnp.int32, (rank, rank), 1
    )
    diagonal = jnp.where(eye, gram, 0.0)
    down = lax.rsqrt(jnp.sum(diagonal, axis=1, keepdims=True))
    along = lax.rsqrt(jnp.sum(diagonal, axis=0, keepdims=True))
    gram = gram * down * along
    start = jnp.where(eye, along, 0.0)
    count = rank // panel
    rows = [gram[i * panel : (i + 1) * panel] for i in range(count)]
    sides = [start[i * panel : (i + 1) * panel] for i in range(count)]
    sub = lax.broadcasted_iota(jnp.int32, (panel, rank), 0)
    finished = []
    for top in range(count):
        first = top * panel
        spread = {
            i: [
                jnp.broadcast_to(rows[i][:, first + k : first + k + 1], (panel, rank))
                for k in range(panel)
            ]
            for i in range(top, count)
        }
        done = jnp.zeros((panel, rank), jnp.float32)
        for j in range(0, panel, 2):
            row0, row1 = rows[top][j : j + 1], rows[top][j + 1 : j + 2]
            side0, side1 = sides[top][j : j + 1], sides[top][j + 1 : j + 2]
            lead_columns = spread[top]
            a = lead_columns[j][j : j + 1]
            b = lead_columns[j][j + 1 : j + 2]
            c = lead_columns[j + 1][j + 1 : j + 2]
            over = reciprocal(a * c - b * b)
            a_over, b_over, c_over = a * over, b * over, c * over
            root = lax.rsqrt(a)
            ratio = b * root * root
            done = jnp.where(sub == j, side0 * root, done)
            done = jnp.where(
                sub == j + 1, (side1 - ratio * side0) * lax.rsqrt(c - ratio * b), done
            )
            heads = [
                (lead_columns[m][j : j + 1], lead_columns[m][j + 1 : j + 2]) for m in range(panel)
            ]
            for i in range(top, count):
                x0, x1 = spread[i][j], spread[i][j + 1]
                m0 = x0 * c_over - x1 * b_over
                m1 = x1 * a_over - x0 * b_over
                rows[i] = rows[i] - (m0 * row0 + m1 * row1)
                sides[i] = sides[i] - (m0 * side0 + m1 * side1)
                for m in range(j + 2, panel):
                    head0, head1 = heads[m]
                    spread[i][m] = spread[i][m] - (m0 * head0 + m1 * head1)
        finished.append(done)
    return jnp.concatenate(finished, axis=0)


def factor(line, gram):
    def kernel(line_ref, gram_ref, out_ref):
        out_ref[...] = inverse_factor(gram_ref[...])

    return small_kernel(kernel, f32(*gram.shape), (line, gram), "factor")


def both_factors(line, bits, gram, theirs, first):
    rank = gram.shape[1]
    half = rank // 2

    def exact(a, b, dims):
        return lax.dot_general(
            a, b, dims, precision=lax.Precision.HIGHEST, preferred_element_type=jnp.float32
        )

    def kernel(line_ref, gram_ref, theirs_ref, first_ref, out_ref, buf):
        side = line_ref[0, bits[0]]
        buf[pl.ds(pl.multiple_of(side * half, 8), half), :] = gram_ref[...]
        buf[pl.ds(pl.multiple_of((1 - side) * half, 8), half), :] = theirs_ref[...]
        first = first_ref[...]
        second_gram = exact(exact(first, buf[...], inner), first, trail)
        out_ref[...] = exact(inverse_factor(second_gram), first, inner)

    return pl.pallas_call(
        kernel,
        out_shape=f32(rank, rank),
        in_specs=[in_smem] + [in_vmem] * 3,
        out_specs=in_vmem,
        scratch_shapes=[pltpu.VMEM((rank, rank), jnp.float32)],
        compiler_params=params,
        name="both_factors",
    )(line, gram, theirs, first)


def finish(line, factors, applied):
    def kernel(line_ref, factors_ref, applied_ref, out_ref):
        out_ref[...] = dot3(applied_ref[...], factors_ref[...], trail)

    return small_kernel(kernel, f32(*applied.shape), (line, factors, applied), "finish")


def covariance_part(line, numbers, prior_cov, snapshots, blocks, filled, carry=False):
    rows, _ = prior_cov.shape
    windows, _, snap_count = snapshots.shape
    count = len(blocks)
    more = [] if filled is None else [filled]
    copied = count if carry else 0
    inv_snap = 1.0 / snap_count

    def kernel(line_ref, cov_ref, snap_ref, *refs):
        block_refs, refs = refs[:count], refs[count + len(more) :]
        out_ref, copy_refs, refs = refs[0], refs[1 : 1 + copied], refs[1 + copied :]
        out_bufs, sems = refs[:-1], refs[-1]
        for block_ref, copy_ref in zip(block_refs, copy_refs):
            copy_ref[...] = block_ref[...]
        copies = []
        for at in range(count):
            width = block_refs[at].shape[1]
            first = pl.multiple_of(line_ref[0, numbers[at]], 128)
            columns = pl.ds(first, width)
            total = cov_ref[:, columns] * forget_factor**windows
            for w in range(windows):
                weight = forget_factor ** (windows - 1 - w) * inv_snap
                total = total + weight * dot(snap_ref[w], block_refs[at][w], trail)
            out_bufs[at][...] = total
            copy = pltpu.make_async_copy(out_bufs[at], out_ref.at[:, columns], sems.at[at])
            copy.start()
            copies.append(copy)
        for copy in copies:
            copy.wait()

    result = pl.pallas_call(
        kernel,
        out_shape=(f32(*prior_cov.shape),)
        + tuple(jax.ShapeDtypeStruct(b.shape, b.dtype) for b in blocks[:copied]),
        in_specs=[in_smem] + [in_vmem] * (2 + count) + [in_hbm] * len(more),
        out_specs=(in_hbm,) + (in_vmem,) * copied,
        scratch_shapes=[pltpu.VMEM((rows, b.shape[1]), jnp.float32) for b in blocks]
        + [pltpu.SemaphoreType.DMA((count,))],
        input_output_aliases={3 + count: 0} if more else {},
        compiler_params=params,
        name="covariance_part",
    )(line, prior_cov, snapshots, *blocks, *more)
    return (result[0], list(result[1:])) if carry else result[0]


def local(devices, prior_cov, snapshots, prior_basis):
    rows = prior_cov.shape[0]
    rank = prior_basis.shape[1]
    windows, _, snap_count = snapshots.shape
    table = ring_table(devices, rows)
    me = lax.axis_index("row")
    line = lax.dynamic_slice_in_dim(jnp.asarray(table), me, 1, axis=0)
    entries = table.shape[1]
    bits = (entries - 2, entries - 1)
    steps = devices // 4
    starts = [0] + [2 + 4 * at for at in range(steps)]
    swap = partner_pairs(devices, 1)

    def fill(filled, numbers):
        blocks = [b for group in snap_ring.groups for b in group]
        chosen = [blocks[n] for n in numbers]
        return covariance_part(line, numbers, prior_cov, snapshots, chosen, filled)

    def fill_own(filled, blocks, numbers):
        return covariance_part(line, numbers, prior_cov, snapshots, blocks, filled, True)

    end = 4 * steps
    snap_ring = Ring(snapshots, devices)
    snap_ring.step()
    mine, theirs, snapshots, values = first_sums(line, bits, snapshots, prior_basis)
    share = new_cov = None
    for window in range(windows):
        got = lax.ppermute(theirs, "row", swap)
        if window == 1:
            (values,) = gate_all([snap_ring], [values])
        ring = Ring(pack(line, values, mine, got, share), devices)
        sum_rows = mine.shape[0]
        state = None
        for phase in range(1, steps + 1):
            if phase == steps:
                ready = state[0]
            sent = ring.recent
            ring.step()
            arrived, ring.recent = ring.recent, sent
            ring.pass_on()
            extra, waiting, filled = [], [ring], []
            if phase == 1:
                waiting.append(snap_ring)
                if window == 0:
                    next_share, snap_copy = local_trace(line, prior_cov, snapshots, sent[0])
                    arrived = gate(arrived, [next_share])
                    extra = [snap_copy]
                else:
                    snap_ring.recent = gate(snap_ring.recent, [sent[0]])
                    snap_ring.pass_on()
                    arrived = gate(arrived)
                    filled = [3, 5, 6, 8]
            else:
                state, _ = product_part(
                    line,
                    starts[phase - 2],
                    prior_cov,
                    ring.groups[phase - 2],
                    state,
                    sum_rows,
                    share,
                    [],
                )
                arrived = gate(arrived, [state[0]])
                extra += state
                if window == 0 and phase == 2:
                    snap_ring.full = [snap_copy]
                    snap_ring.pass_on_full()
                    snap_ring.groups[0][0] = snapshots
                    waiting.append(snap_ring)
                if window == 0 and phase == 3:
                    filled = [0, 1]
                if window == 1 and phase == 2:
                    filled = [7, 9]
            if filled:
                new_cov = fill(new_cov, filled)
                extra.append(new_cov)
            ring.recent = arrived
            if phase == steps and window == 1:
                snap_ring.new_recent = True
                waiting.append(snap_ring)
            if phase == steps and window == 0:
                snap_ring.recent = gate(snap_ring.recent, [ready])
                snap_ring.step()
                if window == 0:
                    new_cov, copies = fill_own(new_cov, snap_ring.full, [2, 4])
                    extra += copies + [new_cov]
                    filled = [2, 4]
            extra = gate_all(waiting, extra)
            if window == 0 and phase == 1:
                snap_copy = extra.pop()
            if filled:
                new_cov = extra.pop()
            if window == 0 and phase == steps:
                extra, copies = extra[:-2], extra[-2:]
            state = extra or None
        if window == 0:
            snap_ring.pass_on_full(copies)
        else:
            snap_ring.step()
        state, _ = product_part(
            line,
            starts[steps - 1],
            prior_cov,
            ring.groups[steps - 1],
            state,
            sum_rows,
            share,
            [],
        )
        ring.pass_on()
        result = product_end(
            line,
            bits,
            starts[steps],
            prior_cov,
            ring.groups[steps],
            state,
            snapshots,
            window,
            share,
        )
        if window == 0:
            (values,) = result
            share = next_share
            mine, theirs = window_sums(line, bits, values, snapshots)
    applied, mine, theirs, first_gram = result
    total = Total(line, bits, mine, theirs, devices, False)
    total.rounds.pop()
    total.round(2)
    first = factor(line, first_gram)
    while snap_ring.done < steps - 1:
        (first,) = gate_all([total, snap_ring], [first])
        snap_ring.pass_on()
        snap_ring.step()
    (first, new_cov) = gate_all([total, snap_ring], [first, new_cov])

    snap_ring.step()
    snap_ring.pass_on_full()
    if end > 16:
        new_cov = fill(new_cov, range(10, end - 6))
    new_cov = fill(new_cov, [end - 6, end - 4])
    blocks = [b for group in snap_ring.groups for b in group]
    new_cov, copies = fill_own(new_cov, [blocks[end - 5], blocks[end - 3]], [end - 5, end - 3])
    total.round(event=copies[0])
    (first, new_cov) = gate_all([total, snap_ring], [first, new_cov])
    snap_ring.pass_on()
    blocks = [b for group in snap_ring.groups for b in group]
    new_cov, copies = fill_own(new_cov, blocks[end - 2 : end], [end - 2, end - 1])
    while total.rounds:
        total.round(event=copies[0])
    (first, new_cov) = gate_all([total], [first, new_cov])
    theirs = lax.ppermute(total.mine, "row", swap)
    factors = both_factors(line, bits, total.mine, theirs, first)
    new_basis = finish(line, factors, applied)
    return (new_cov, new_basis)


def solution(mesh):
    return jax.shard_map(
        functools.partial(local, mesh.shape["row"]),
        mesh=mesh,
        in_specs=(
            P(("band", "row"), None),
            P(None, ("band", "row"), None),
            P(("band", "row"), None),
        ),
        out_specs=(P(("band", "row"), None), P(("band", "row"), None)),
        check_vma=False,
    )
```
